256 devices in a mesh: view: 16 (over z_lo, x, core), render: 4 (over z_hi), head: 4 (over y).
Axes of the slice: x: 4, y: 4, z: 8 (z_hi: 4, z_lo: 2; z = z_hi * 2 + z_lo), core: 2. Of those that a mesh axis runs over, the one named last changes fastest.
Arguments:
- input_keys: bfloat16 [16384, 4096], P('view', 'head'), may hold values from -6 to 6
- input_values: bfloat16 [16384, 4096], P('view', 'head'), may hold values from -6 to 6
- token_rates: float32 [4, 16384], P('head', 'view'), may hold values from 0.00015625 to 0.0015625
- gate_weight: bfloat16 [4, 1024, 2048], P('head', None, 'render'), may hold values from -1.25 to 1.25
- up_weight: bfloat16 [4, 1024, 2048], P('head', None, 'render'), may hold values from -1.25 to 1.25
- down_weight: bfloat16 [4, 1024, 2048], P('head', None, 'render'), may hold values from -0.8838835 to 0.8838835
- queries: bfloat16 [16384, 4096], P(('view', 'render'), 'head'), may hold values from -6 to 6
Outputs:
- rendered: bfloat16 [16384, 4096], P(('view', 'render'), 'head')
The draws below stay inside these ranges and needn't reach their ends.
All inputs are finite; a program needn't handle non-finite values.
Results may differ from the reference program's by a relative error of at most 0.04.
Values may be sent and summed in bfloat16 or wider, within the bound.
No kernel may reach another device: no remote copies, remote signals or barrier semaphores. Data moves between devices by JAX's collectives and lax.ppermute only.
A program may use at most 64 MiB of HBM per device.

```python
import math
import jax
import jax.numpy as jnp
from jax import lax

HW = 1024
FH = 2048
HEADS = 4
TIN = 16384
QTOK = 16384


def scaled_weight(key, fan, col_low, col_high):
    noise_key = jax.random.fold_in(key, 0)
    col_key = jax.random.fold_in(key, 2)
    row_key = jax.random.fold_in(key, 3)
    shape = (HEADS, HW, FH)
    normal_part = jnp.clip(jax.random.normal(noise_key, shape, jnp.float32), -5.0, 5.0)
    base = normal_part
    col_scale = jnp.exp(jax.random.uniform(col_key, (HEADS, 1, FH), jnp.float32, jnp.log(col_low), jnp.log(col_high)))
    row_scale = jnp.exp(jax.random.uniform(row_key, (HEADS, HW, 1), jnp.float32, jnp.log(0.5), jnp.log(2.0)))
    return (base * col_scale * row_scale / jnp.sqrt(jnp.float32(fan))).astype(jnp.bfloat16)


def draw_gate_weight(key, part):
    key = jax.random.fold_in(key, 11)
    return scaled_weight(key, HW, 0.9, 1.1)


def draw_up_weight(key, part):
    key = jax.random.fold_in(key, 23)
    return scaled_weight(key, HW, 0.9, 1.1)


def draw_down_weight(key, part):
    key = jax.random.fold_in(key, 37)
    return scaled_weight(key, FH, 0.9, 1.1)


def levels(own_key, shape, pieces, low, top_value):
    def one(axis_at, blocks):
        steps = jax.random.uniform(jax.random.fold_in(jax.random.fold_in(own_key, 6), axis_at), (blocks,), jnp.float32, low / len(pieces), top_value / len(pieces))
        return jnp.repeat(jnp.exp(steps), shape[axis_at] // blocks).reshape((-1,) + (1,) * (len(shape) - axis_at - 1))

    level = one(*pieces[0])
    for cut in pieces[1:]:
        level = level * one(*cut)
    return level


def noise(stream_key, shape, width, bound, shards=(), held_as=jnp.bfloat16):
    level = levels(stream_key, shape, shards, -0.22, 0.18) if shards else 1.0
    values = jax.random.normal(stream_key, shape, jnp.float32) * width * level
    return jnp.minimum(jnp.maximum(values, -bound), bound).astype(held_as)


def setup_inputs(seed: int = 0) -> dict:
    splits = jax.random.split(jax.random.key(seed), 8)
    input_keys = noise(splits[0], (TIN, HEADS * HW), 1.0, 6.0, ((0, 16), (1, 4)))
    input_values = noise(splits[1], (TIN, HEADS * HW), 1.0, 6.0, ((0, 16), (1, 4)))
    token_rates = jnp.clip(jnp.exp(math.log(0.0015625) - 2.3025851 * jax.random.uniform(splits[2], (HEADS, TIN), jnp.float32) ** levels(splits[2], (HEADS, TIN), ((0, 4), (1, 16)), -0.2, 0.2)), 0.00015625, 0.0015625)
    gate_weight = draw_gate_weight(jax.random.fold_in(splits[7], 71), 0)
    up_weight = draw_up_weight(jax.random.fold_in(splits[7], 71), 0)
    down_weight = draw_down_weight(jax.random.fold_in(splits[7], 71), 0)
    queries = noise(splits[6], (QTOK, HEADS * HW), 1.0, 6.0, ((0, 64), (1, 4)))
    return {"input_keys": input_keys, "input_values": input_values, "token_rates": token_rates, "gate_weight": gate_weight, "up_weight": up_weight, "down_weight": down_weight, "queries": queries}


def renorm(old, delta):
    old_wide = old.astype(jnp.float32)
    summed = old_wide + delta
    factor = jnp.sqrt(lax.optimization_barrier(jnp.sum(old_wide * old_wide, axis=-2, keepdims=True))) / jnp.sqrt(lax.optimization_barrier(jnp.sum(summed * summed, axis=-2, keepdims=True)) + 1e-06)
    return (summed * factor).astype(jnp.bfloat16)

def contract_rows(left, right):
    return lax.dot_general(left, right, (((0,), (0,)), ((), ())), preferred_element_type=jnp.float32)

def reference(input_keys, input_values, token_rates, gate_weight, up_weight, down_weight, queries):

    def one_head(head):
        offset = (head * HW).astype(jnp.int32)
        key_cols = lax.dynamic_slice_in_dim(input_keys, offset, HW, 1)
        value_cols = lax.dynamic_slice_in_dim(input_values, offset, HW, 1)
        query_cols = lax.dynamic_slice_in_dim(queries, offset, HW, 1)
        rate_col = lax.dynamic_index_in_dim(token_rates, head, 0, keepdims=False)[:, None]
        old_gate = lax.dynamic_index_in_dim(gate_weight, head, 0, keepdims=False)
        old_up = lax.dynamic_index_in_dim(up_weight, head, 0, keepdims=False)
        old_down = lax.dynamic_index_in_dim(down_weight, head, 0, keepdims=False)
        gate_out = jnp.dot(key_cols, old_gate, preferred_element_type=jnp.float32)
        up_out = jnp.dot(key_cols, old_up, preferred_element_type=jnp.float32)
        back_grad = jnp.dot(value_cols, old_down, preferred_element_type=jnp.float32)
        sigmoid_gate = jax.nn.sigmoid(gate_out)
        activated = gate_out * sigmoid_gate
        hidden = (activated * up_out).astype(jnp.bfloat16)
        scaled_values = (rate_col * value_cols.astype(jnp.float32)).astype(jnp.bfloat16)
        pre_gate = (rate_col * back_grad * up_out * sigmoid_gate * (1.0 + gate_out * (1.0 - sigmoid_gate))).astype(jnp.bfloat16)
        pre_up = (rate_col * back_grad * activated).astype(jnp.bfloat16)
        new_gate = renorm(old_gate, contract_rows(key_cols, pre_gate))
        new_up = renorm(old_up, contract_rows(key_cols, pre_up))
        new_down = renorm(old_down, contract_rows(scaled_values, hidden))
        gate_q = jnp.dot(query_cols, new_gate, preferred_element_type=jnp.float32)
        up_q = jnp.dot(query_cols, new_up, preferred_element_type=jnp.float32)
        hidden_q = (gate_q * jax.nn.sigmoid(gate_q) * up_q).astype(jnp.bfloat16)
        result = lax.dot_general(hidden_q, new_down, (((1,), (1,)), ((), ())), preferred_element_type=jnp.float32)
        return result.astype(jnp.bfloat16)
    stacked = lax.map(one_head, jnp.arange(HEADS, dtype=jnp.int32))
    return jnp.transpose(stacked, (1, 0, 2)).reshape(QTOK, HEADS * HW)
```

```python
import jax
import jax.numpy as jnp
from jax import lax
from jax.sharding import PartitionSpec as P

AXES = ("view", "render")
LZ, NX, NC, HZ = 2, 4, 2, 4
NZ = LZ * HZ
F32 = jnp.float32
BF16 = jnp.bfloat16


def move(array, target):
    pairs = []
    for zl in range(LZ):
        for x in range(NX):
            for core in range(NC):
                for zh in range(HZ):
                    tl, tx, tc, th = target(zl, x, core, zh)
                    pairs.append(
                        (((zl * NX + x) * NC + core) * HZ + zh, ((tl * NX + tx) * NC + tc) * HZ + th)
                    )
    return lax.ppermute(array, AXES, pairs)


def along_x(array, step):
    return move(array, lambda zl, x, c, zh: (zl, (x + step) % NX, c, zh))


def along_z(array, step):
    def target(zl, x, c, zh):
        z = (zh * LZ + zl + step) % NZ
        return z % LZ, x, c, z // LZ

    return move(array, target)


def swap_core(array):
    return move(array, lambda zl, x, c, zh: (zl, x, 1 - c, zh))


def swap_pair(array):
    return move(array, lambda zl, x, c, zh: (1 - zl, x, c, zh))


def pick(array, index, axis=0):
    return lax.dynamic_index_in_dim(array, index, axis, keepdims=False)


def add(*terms):
    total = terms[0].astype(F32)
    for term in terms[1:]:
        total = total + term.astype(F32)
    return total


def local(input_keys, input_values, token_rates, gate_weight, up_weight, down_weight, queries):
    view = lax.axis_index("view")
    zl, x, core = view // (NX * NC), (view // NC) % NX, view % NC
    tokens, width = input_keys.shape
    units = gate_weight.shape[2]
    own_units = units // (NC * NX * LZ)

    rate_col = token_rates[0][:, None]
    gate_out = jnp.dot(input_keys, gate_weight[0], preferred_element_type=F32)
    up_out = jnp.dot(input_keys, up_weight[0], preferred_element_type=F32)
    sigmoid_gate = jax.nn.sigmoid(gate_out)
    activated = gate_out * sigmoid_gate
    hidden = (activated * up_out).astype(BF16)
    scaled_values = (rate_col * input_values.astype(F32)).astype(BF16)
    back_grad = jnp.dot(input_values, down_weight[0], preferred_element_type=F32)
    pre_gate = (
        rate_col * back_grad * up_out * sigmoid_gate * (1.0 + gate_out * (1.0 - sigmoid_gate))
    ).astype(BF16)
    pre_up = (rate_col * back_grad * activated).astype(BF16)

    def delta(left, right):
        full = lax.dot_general(left, right, (((0,), (0,)), ((), ())), preferred_element_type=F32)
        return full.reshape(NC, NX, LZ, own_units, width).astype(BF16)

    def reduce_x(part):
        mine = pick(part, core)
        chip = add(mine, swap_core(pick(part, 1 - core))).astype(BF16)
        got = [along_x(pick(chip, (x + step) % NX), step) for step in (2, 1, 3)]
        return add(pick(chip, x), *got)

    sums = [
        reduce_x(delta(hidden, scaled_values)),
        reduce_x(delta(pre_gate, input_keys)),
        reduce_x(delta(pre_up, input_keys)),
    ]
    both = jnp.stack([sums[1], sums[2], sums[0]], 1).astype(BF16)
    mine = add(pick(both, zl), swap_pair(pick(both, 1 - zl)))

    offset = ((core * NX + x) * LZ + zl) * own_units
    old = jnp.stack(
        [
            lax.dynamic_slice_in_dim(w[0], offset, own_units, 1).T
            for w in (gate_weight, up_weight, down_weight)
        ]
    ).astype(F32)
    summed = old + mine
    factor = jnp.sqrt(jnp.sum(old * old, axis=-1, keepdims=True)) / jnp.sqrt(
        jnp.sum(summed * summed, axis=-1, keepdims=True) + 1e-06
    )
    new = (summed * factor).astype(BF16)

    pieces = [new]
    up_way, down_way = new, new
    for _ in range(NZ // 2 - 1):
        up_way, down_way = along_z(up_way, 1), along_z(down_way, -1)
        pieces += [up_way, down_way]
    half = own_units // 2
    pieces.append(
        jnp.concatenate([along_z(up_way[:, :half], 1), along_z(down_way[:, half:], -1)], 1)
    )
    here = jnp.concatenate(pieces, 1)
    weights = jnp.concatenate([here, swap_core(here)], 1)

    query_rows = [queries] + [along_x(queries, -step) for step in (2, 1, 3)]
    outs = []
    for rows in query_rows:
        gate_q = lax.dot_general(rows, weights[0], (((1,), (1,)), ((), ())), preferred_element_type=F32)
        up_q = lax.dot_general(rows, weights[1], (((1,), (1,)), ((), ())), preferred_element_type=F32)
        hidden_q = (gate_q * jax.nn.sigmoid(gate_q) * up_q).astype(BF16)
        outs.append(jnp.dot(hidden_q, weights[2], preferred_element_type=F32))
    got = [along_x(out.astype(BF16), step) for out, step in zip(outs[1:], (2, 1, 3))]
    return add(outs[0], *got).astype(BF16)


def solution(mesh):
    return jax.shard_map(
        local,
        mesh=mesh,
        in_specs=(
            P("view", "head"),
            P("view", "head"),
            P("head", "view"),
            P("head", None, "render"),
            P("head", None, "render"),
            P("head", None, "render"),
            P(("view", "render"), "head"),
        ),
        out_specs=P(("view", "render"), "head"),
        check_vma=False,
    )
```

```python
import functools

import jax
import jax.numpy as jnp
from jax import lax
from jax.experimental import pallas as pl
from jax.experimental.pallas import tpu as pltpu
from jax.sharding import PartitionSpec as P

AXES = ("view", "render")
LZ, NX, NC, HZ = 2, 4, 2, 4
NZ = LZ * HZ
F32 = jnp.float32
BF16 = jnp.bfloat16
VMEM_BYTES = 48 * 1024 * 1024
OTHERS = ((2, 1), (1, 1), (3, 1), (2, 0), (1, 0), (3, 0), (0, 1))


def move(array, target):
    pairs = []
    for zl in range(LZ):
        for x in range(NX):
            for core in range(NC):
                for zh in range(HZ):
                    tl, tx, tc, th = target(zl, x, core, zh)
                    pairs.append(
                        (((zl * NX + x) * NC + core) * HZ + zh, ((tl * NX + tx) * NC + tc) * HZ + th)
                    )
    return lax.ppermute(array, AXES, pairs)


def along_x(array, step):
    return move(array, lambda zl, x, c, zh: (zl, (x + step) % NX, c, zh))


def along_z(array, step):
    def target(zl, x, c, zh):
        z = (zh * LZ + zl + step) % NZ
        return z % LZ, x, c, z // LZ

    return move(array, target)


def to_owner(array, step_x, step_zl):
    return move(array, lambda zl, x, c, zh: ((zl + step_zl) % LZ, (x + step_x) % NX, c, zh))


def swap_core(array):
    return move(array, lambda zl, x, c, zh: (zl, x, 1 - c, zh))


def contract(left, right, left_dim, right_dim):
    return lax.dot_general(
        left, right, (((left_dim,), (right_dim,)), ((), ())), preferred_element_type=F32
    )


def params():
    return pltpu.CompilerParams(vmem_limit_bytes=VMEM_BYTES)


def delta_kernel(index, keys, values, rates, gate, up, down, out, *old):
    k, v, r = keys[...], values[...], rates[...]
    gate_in = contract(gate[0], k, 0, 1)
    up_in = contract(up[0], k, 0, 1)
    back = contract(down[0], v, 0, 1)
    s = jax.nn.sigmoid(gate_in)
    act = gate_in * s
    hidden = (r * (act * up_in)).astype(BF16)
    rated = r * back
    pre_gate = (rated * up_in * s * (1.0 + gate_in * (1.0 - s))).astype(BF16)
    pre_up = (rated * act).astype(BF16)
    out[0] = contract(pre_gate, k, 1, 0).astype(BF16)
    out[1] = contract(pre_up, k, 1, 0).astype(BF16)
    out[2] = contract(hidden, v, 1, 0).astype(BF16)
    if old:
        rows_out, turned = old
        units = rows_out.shape[1]
        block = pl.multiple_of(index[1], 128)
        row = pl.multiple_of(index[2], units)
        for m, weight in enumerate((gate, up, down)):
            turned[...] = weight[0, :, pl.ds(block, 128)].astype(F32).T
            rows_out[m] = turned[pl.ds(row, units), :]


def deltas(index, keys, values, rates, weights, units, with_old):
    tokens, width = keys.shape
    own = units // (NX * LZ)
    whole = lambda shape: pl.BlockSpec(shape, lambda i, index: (0,) * len(shape))
    column = pl.BlockSpec((1, width, units), lambda i, index: (0, 0, index[0]))
    out_shape = [jax.ShapeDtypeStruct((3, units, width), BF16)]
    scratch = []
    if with_old:
        out_shape.append(jax.ShapeDtypeStruct((3, own, width), F32))
        scratch = [pltpu.VMEM((128, width), F32)]
    return pl.pallas_call(
        delta_kernel,
        name="delta_own" if with_old else "delta_other",
        grid_spec=pltpu.PrefetchScalarGridSpec(
            num_scalar_prefetch=1,
            grid=(1,),
            in_specs=[
                whole((tokens, width)),
                whole((tokens, width)),
                whole((1, tokens)),
                column,
                column,
                column,
            ],
            out_specs=[whole(o.shape) for o in out_shape],
            scratch_shapes=scratch,
        ),
        out_shape=out_shape,
        compiler_params=params(),
        cost_estimate=pl.CostEstimate(
            flops=12 * tokens * width * units, bytes_accessed=8 << 20, transcendentals=tokens * units
        ),
    )(index, keys, values, rates, *weights)


def split_kernel(place, mine, other, keep, *outs):
    x, zl = place[0], place[1]
    own = keep.shape[1]

    def rows(step_x, step_zl):
        start = ((x + step_x) % NX * LZ + (zl + step_zl) % LZ) * own
        part = pl.ds(pl.multiple_of(start, own), own)
        return mine[:, part, :].astype(F32) + other[:, part, :].astype(F32)

    keep[...] = rows(0, 0)
    for out, steps in zip(outs, OTHERS):
        out[...] = rows(*steps).astype(BF16)


def split(place, mine, other):
    _, units, width = mine.shape
    own = units // (NX * LZ)
    vmem = pl.BlockSpec(memory_space=pltpu.VMEM)
    return pl.pallas_call(
        split_kernel,
        name="split",
        in_specs=[pl.BlockSpec(memory_space=pltpu.SMEM), vmem, vmem],
        out_specs=[vmem] * (1 + len(OTHERS)),
        out_shape=[jax.ShapeDtypeStruct((3, own, width), F32)]
        + [jax.ShapeDtypeStruct((3, own, width), BF16)] * len(OTHERS),
        compiler_params=params(),
    )(place, mine, other)


def renorm_kernel(old, keep, *refs):
    out = refs[-1]
    was = old[...]
    summed = keep[...]
    for ref in refs[:-1]:
        summed = summed + ref[...].astype(F32)
    summed = was + summed
    factor = jnp.sqrt(jnp.sum(was * was, axis=-1, keepdims=True)) / jnp.sqrt(
        jnp.sum(summed * summed, axis=-1, keepdims=True) + 1e-06
    )
    out[...] = (summed * factor).astype(BF16)


def renorm(old, keep, got):
    vmem = pl.BlockSpec(memory_space=pltpu.VMEM)
    return pl.pallas_call(
        renorm_kernel,
        name="renorm",
        in_specs=[vmem] * (2 + len(got)),
        out_specs=vmem,
        out_shape=jax.ShapeDtypeStruct(old.shape, BF16),
        compiler_params=params(),
    )(old, keep, *got)


def join_kernel(*refs):
    out = refs[-1]
    at = 0
    for ref in refs[:-1]:
        n = ref.shape[1]
        out[:, at : at + n, :] = ref[...]
        at += n


def join(pieces):
    vmem = pl.BlockSpec(memory_space=pltpu.VMEM)
    units = sum(p.shape[1] for p in pieces)
    return pl.pallas_call(
        join_kernel,
        name="join",
        in_specs=[vmem] * len(pieces),
        out_specs=vmem,
        out_shape=jax.ShapeDtypeStruct((3, units, pieces[0].shape[2]), BF16),
        compiler_params=params(),
    )(*pieces)


def render_kernel(rows, weights, out):
    q = rows[...]
    gate_q = contract(q, weights[0], 1, 1)
    up_q = contract(q, weights[1], 1, 1)
    hidden_q = (gate_q * jax.nn.sigmoid(gate_q) * up_q).astype(BF16)
    out[...] = contract(hidden_q, weights[2], 1, 0).astype(out.dtype)


def render(rows, weights, dtype):
    vmem = pl.BlockSpec(memory_space=pltpu.VMEM)
    n, width = rows.shape
    return pl.pallas_call(
        render_kernel,
        name="render_rows",
        in_specs=[vmem, vmem],
        out_specs=vmem,
        out_shape=jax.ShapeDtypeStruct((n, width), dtype),
        compiler_params=params(),
        cost_estimate=pl.CostEstimate(
            flops=6 * n * width * weights.shape[1],
            bytes_accessed=4 << 20,
            transcendentals=n * weights.shape[1],
        ),
    )(rows, weights)


def total_kernel(*refs):
    total = refs[0][...].astype(F32)
    for ref in refs[1:-1]:
        total = total + ref[...].astype(F32)
    refs[-1][...] = total.astype(BF16)


def total(parts):
    vmem = pl.BlockSpec(memory_space=pltpu.VMEM)
    return pl.pallas_call(
        total_kernel,
        name="total",
        in_specs=[vmem] * len(parts),
        out_specs=vmem,
        out_shape=jax.ShapeDtypeStruct(parts[0].shape, BF16),
        compiler_params=params(),
    )(*parts)


def local(input_keys, input_values, token_rates, gate_weight, up_weight, down_weight, queries):
    view = lax.axis_index("view")
    zl, x, core = view // (NX * NC), (view // NC) % NX, view % NC
    units = gate_weight.shape[2] // NC
    own = units // (NX * LZ)
    start = (x * LZ + zl) * own

    tokens = (input_keys, input_values, token_rates)
    weights = (gate_weight, up_weight, down_weight)
    index = lambda c: jnp.stack([c, start // 128 * 128, start % 128]).astype(jnp.int32)
    (other_units,) = deltas(index(1 - core), *tokens, weights, units, False)
    from_other = swap_core(other_units)
    mine, old = deltas(index(core), *tokens, weights, units, True)
    keep, *sends = split(jnp.stack([x, zl]).astype(jnp.int32), mine, from_other)
    got = [to_owner(s, *steps) for s, steps in zip(sends, OTHERS)]
    queries, *got = lax.optimization_barrier((queries, *got))
    new = renorm(old, keep, got)

    half = own // 2
    right1, right2 = along_z(new, 1), along_z(new, 2)
    left1, left2 = along_z(new, -1), along_z(new, -2)
    right3, left3 = along_z(right2, 1), along_z(left2, -1)
    far = [along_z(right2[:, :half], 2), along_z(left2[:, half:], -2)]
    near = [new, right1, left1, right2, left2]
    pieces = near + [right3, left3] + far
    held = join(pieces + [swap_core(p) for p in pieces])

    asked = [(step, along_x(queries, -step)) for step in (2, 1, 3)]
    got = [along_x(render(rows, held, BF16), step) for step, rows in asked]
    return total([render(queries, held, F32)] + got)


def solution(mesh):
    return jax.shard_map(
        local,
        mesh=mesh,
        in_specs=(
            P("view", "head"),
            P("view", "head"),
            P("head", "view"),
            P("head", None, "render"),
            P("head", None, "render"),
            P("head", None, "render"),
            P(("view", "render"), "head"),
        ),
        out_specs=P(("view", "render"), "head"),
        check_vma=False,
    )
```

```python
import functools

import jax
import jax.numpy as jnp
from jax import lax
from jax.experimental import pallas as pl
from jax.experimental.pallas import tpu as pltpu
from jax.sharding import PartitionSpec as P

AXES = ("view", "render")
LZ, NX, NC, HZ = 2, 4, 2, 4
NZ = LZ * HZ
F32 = jnp.float32
BF16 = jnp.bfloat16
SHORT = pl.CostEstimate(flops=1, bytes_accessed=1, transcendentals=0)


def move(array, target):
    pairs = []
    for zl in range(LZ):
        for x in range(NX):
            for core in range(NC):
                for zh in range(HZ):
                    tl, tx, tc, th = target(zl, x, core, zh)
                    pairs.append(
                        (((zl * NX + x) * NC + core) * HZ + zh, ((tl * NX + tx) * NC + tc) * HZ + th)
                    )
    return lax.ppermute(array, AXES, pairs)


def along_x(array, step):
    return move(array, lambda zl, x, c, zh: (zl, (x + step) % NX, c, zh))


def to_owner(array, step):
    return move(array, lambda zl, x, c, zh: (c, (x + step) % NX, zl, zh))


def along_z(array, step):
    def target(zl, x, c, zh):
        z = (zh * LZ + zl + (1 - 2 * c) * step) % NZ
        return z % LZ, x, c, z // LZ

    return move(array, target)


def swap_core(array):
    return move(array, lambda zl, x, c, zh: (zl, x, 1 - c, zh))


def contract(left, right, left_dim, right_dim):
    return lax.dot_general(
        left, right, (((left_dim,), (right_dim,)), ((), ())), preferred_element_type=F32
    )


def params(mib=32):
    return pltpu.CompilerParams(vmem_limit_bytes=mib * 1024 * 1024)


def delta_kernel(steps, place, rates, keys, values, gate, up, down, mine, other, *refs):
    old = refs[0] if len(refs) > 5 else None
    k_ref, v_ref, columns, turned, sems = refs[-5:]
    x, zl, core = place[0], place[1], place[2]
    units = gate.shape[2] // NX
    half = units // NC
    n = units * len(steps)

    def fetch(m, weight):
        for b, step in enumerate(steps):
            start = pl.multiple_of((x + step) % NX * units, units)
            yield pltpu.make_async_copy(
                weight.at[0, :, pl.ds(start, units)],
                columns.at[m, :, b * units : (b + 1) * units],
                sems.at[2 + m * len(steps) + b],
            )

    copies = [pltpu.make_async_copy(keys, k_ref, sems.at[0]), *fetch(0, gate), *fetch(1, up)]
    later = [pltpu.make_async_copy(values, v_ref, sems.at[1]), *fetch(2, down)]
    for copy in copies + later:
        copy.start()
    for copy in copies:
        copy.wait()
    k = k_ref[...]
    both = contract(jnp.concatenate([columns[0], columns[1]], 1), k, 0, 1)
    gate_in, up_in = both[:n], both[n:]
    for copy in later:
        copy.wait()
    v, r = v_ref[...], rates[...]
    back = contract(columns[2], v, 0, 1)
    s = jax.nn.sigmoid(gate_in)
    act = gate_in * s
    rated = r * back
    turned[0] = (rated * up_in * s * (1.0 + gate_in * (1.0 - s))).astype(BF16)
    turned[1] = (rated * act).astype(BF16)
    turned[2] = (r * (act * up_in)).astype(BF16)
    parts = [(c, b) for c in (1 - core, core) for b in range(len(steps))]
    rows = [pl.ds(pl.multiple_of(b * units + c * half, half), half) for c, b in parts]
    pres = jnp.concatenate([turned[m, part] for part in rows for m in (0, 1)], 0)
    key_sums = contract(pres, k, 1, 0).astype(BF16)
    value_sums = contract(jnp.concatenate([turned[2, part] for part in rows], 0), v, 1, 0).astype(BF16)
    for i in range(len(parts)):
        out, b = (other, mine)[i // len(steps)], i % len(steps)
        out[b, 0] = key_sums[2 * i * half : (2 * i + 1) * half]
        out[b, 1] = key_sums[(2 * i + 1) * half : (2 * i + 2) * half]
        out[b, 2] = value_sums[i * half : (i + 1) * half]
    if old is not None:
        old_turned = refs[1]
        own = pl.ds(pl.multiple_of(zl * half, half), half)
        for m in range(3):
            old_turned[...] = columns[m, :, (len(steps) - 1) * units :].astype(F32).T
            old[m] = old_turned[own, :]


def deltas(place, steps, rates, arrays):
    count, width = arrays[0].shape
    units = arrays[2].shape[2] // NX
    half = units // NC
    n = units * len(steps)
    vmem = pl.BlockSpec(memory_space=pltpu.VMEM)
    out_shape = [jax.ShapeDtypeStruct((len(steps), 3, half, width), BF16)] * 2
    scratch = [
        pltpu.VMEM((count, width), BF16),
        pltpu.VMEM((count, width), BF16),
        pltpu.VMEM((3, width, n), BF16),
        pltpu.VMEM((3, n, count), BF16),
        pltpu.SemaphoreType.DMA((2 + 3 * len(steps),)),
    ]
    if steps[-1] == 0:
        out_shape.append(jax.ShapeDtypeStruct((3, half, width), F32))
        scratch = [pltpu.VMEM((units, width), F32)] + scratch
    return pl.pallas_call(
        functools.partial(delta_kernel, steps),
        name="delta_%d%d" % steps,
        in_specs=[pl.BlockSpec(memory_space=pltpu.SMEM), vmem]
        + [pl.BlockSpec(memory_space=pl.ANY)] * len(arrays),
        out_specs=[vmem] * len(out_shape),
        out_shape=out_shape,
        scratch_shapes=scratch,
        compiler_params=params(52),
        cost_estimate=SHORT,
    )(place, rates, *arrays)


def call(kernel, name, out_shape, *operands):
    vmem = pl.BlockSpec(memory_space=pltpu.VMEM)
    return pl.pallas_call(
        kernel,
        name=name,
        in_specs=[pl.BlockSpec(memory_space=pltpu.SMEM) if o.ndim == 1 else vmem for o in operands],
        out_specs=jax.tree.map(lambda _: vmem, out_shape),
        out_shape=out_shape,
        compiler_params=params(),
        cost_estimate=SHORT,
    )(*operands)


def add_kernel(mine, other, *outs):
    for i, out in enumerate(outs):
        out[...] = (mine[i].astype(F32) + other[i].astype(F32)).astype(out.dtype)


def add_cores(mine, other):
    block = jax.ShapeDtypeStruct(mine.shape[1:], BF16)
    return call(add_kernel, "add_cores", [block] * mine.shape[0], mine, other)


def sum_kernel(*refs):
    sums = refs[0][...].astype(F32)
    for ref in refs[1:-1]:
        sums = sums + ref[...].astype(F32)
    refs[-1][...] = sums.astype(refs[-1].dtype)


def add_up(name, parts):
    return call(sum_kernel, name, jax.ShapeDtypeStruct(parts[0].shape, BF16), *parts)


def renorm_kernel(place, old, mine, other, out):
    half = out.shape[1] // 2
    was = old[...]
    summed = was + (mine[...].astype(F32) + other[...].astype(F32))
    factor = jnp.sqrt(jnp.sum(was * was, axis=-1, keepdims=True)) / jnp.sqrt(
        jnp.sum(summed * summed, axis=-1, keepdims=True) + 1e-06
    )
    new = (summed * factor).astype(BF16)
    core = place[2]
    for i in range(2):
        at = pl.multiple_of((core + i) % 2 * half, half)
        out[:, pl.ds(at, half), :] = new[:, i * half : (i + 1) * half]


def join_kernel(*refs):
    out = refs[-1]
    at = 0
    for ref in refs[:-1]:
        n = ref.shape[1]
        out[:, at : at + n, :] = ref[...]
        at += n


def join(pieces):
    units = sum(p.shape[1] for p in pieces)
    out = jax.ShapeDtypeStruct((3, units, pieces[0].shape[2]), BF16)
    return call(join_kernel, "join", out, *pieces)


def render_kernel(cuts, *refs):
    rows, pieces, out = refs[: len(cuts)], refs[len(cuts) : -1], refs[-1]
    gate, up, down = (jnp.concatenate([p[m] for p in pieces], 0) for m in range(3))
    q = jnp.concatenate([ref[lo:hi, :] for ref, (lo, hi) in zip(rows, cuts)], 0)
    gate_q = contract(q, gate, 1, 1)
    up_q = contract(q, up, 1, 1)
    hidden_q = (gate_q * jax.nn.sigmoid(gate_q) * up_q).astype(BF16)
    out[...] = contract(hidden_q, down, 1, 0).astype(out.dtype)


def render(rows, pieces, dtype):
    cuts = tuple((lo, hi) for _, lo, hi in rows)
    out = jax.ShapeDtypeStruct((sum(hi - lo for lo, hi in cuts), pieces[0].shape[2]), dtype)
    kernel = functools.partial(render_kernel, cuts)
    return call(kernel, "render_rows", out, *[r[0] for r in rows], *pieces)


def merge_kernel(mid, from_left, from_right, to_right, to_left):
    half = to_right.shape[0]
    to_right[...] = (mid[:half] + from_left[:half].astype(F32)).astype(BF16)
    to_left[...] = (mid[half:] + from_right[:half].astype(F32)).astype(BF16)


def total_kernel(own, from_left, from_right, last_left, last_right, out):
    half = last_left.shape[0]
    top = own[:half] + from_right[half:].astype(F32) + last_left[...].astype(F32)
    low = own[half:] + from_left[half:].astype(F32) + last_right[...].astype(F32)
    out[:half] = top.astype(BF16)
    out[half:] = low.astype(BF16)


def local(input_keys, input_values, token_rates, gate_weight, up_weight, down_weight, queries):
    view = lax.axis_index("view")
    zl, x, core = view // (NX * NC), (view // NC) % NX, view % NC
    place = jnp.stack([x, zl, core]).astype(jnp.int32)

    arrays = (input_keys, input_values, gate_weight, up_weight, down_weight)
    mine, other = deltas(place, (2, 1), token_rates, arrays)
    first = swap_core(other)
    second_mine, other, old = deltas(place, (3, 0), token_rates, arrays)
    chip2, chip1 = add_cores(mine, first)
    got2, got1 = to_owner(chip2, 2), to_owner(chip1, 1)
    chip3, chip0 = add_cores(second_mine, swap_core(other))
    got3, got0 = to_owner(chip3, 3), to_owner(chip0, 0)
    sums = add_up("sum_chips", [got2, got1, got3, got0])
    sums, queries = lax.optimization_barrier((sums, queries))
    out = jax.ShapeDtypeStruct(old.shape, BF16)
    new = call(renorm_kernel, "renorm", out, place, old, sums, swap_core(sums))

    half = queries.shape[0] // 2
    from_right, from_left = along_x(queries, -1), along_x(queries, 1)
    near1, near2 = along_z(new, 1), along_z(new, 2)
    near1, near2, from_right, from_left = lax.optimization_barrier((near1, near2, from_right, from_left))
    far_top, far_low = along_x(from_right[:half], -1), along_x(from_left[half:], 1)
    third, fourth = along_z(near2, 1), along_z(near2[:, : new.shape[1] // 2], 2)
    near = join([near1, near2])
    near_other = swap_core(near)
    third, fourth, far_top, far_low, near_other = lax.optimization_barrier(
        (third, fourth, far_top, far_low, near_other)
    )
    last = join([third, fourth])
    pieces = [new, near, near_other, last, swap_core(last)]

    both = 2 * half
    to_right = render([(far_top, 0, half), (from_right, half, both)], pieces, BF16)
    to_left = render([(far_low, 0, half), (from_left, 0, half)], pieces, BF16)
    got_left, got_right = along_x(to_right, 1), along_x(to_left, -1)
    mid = render([(from_right, 0, half), (from_left, half, both)], pieces, F32)
    own = render([(queries, 0, both)], pieces, F32)
    part = jax.ShapeDtypeStruct((half, own.shape[1]), BF16)
    to_right, to_left = call(merge_kernel, "merge", [part] * 2, mid, got_left, got_right)
    last_left, last_right = along_x(to_right, 1), along_x(to_left, -1)
    out = jax.ShapeDtypeStruct(own.shape, BF16)
    return call(total_kernel, "total", out, own, got_left, got_right, last_left, last_right)


def solution(mesh):
    return jax.shard_map(
        local,
        mesh=mesh,
        in_specs=(
            P("view", "head"),
            P("view", "head"),
            P("head", "view"),
            P("head", None, "render"),
            P("head", None, "render"),
            P("head", None, "render"),
            P(("view", "render"), "head"),
        ),
        out_specs=P(("view", "render"), "head"),
        check_vma=False,
    )
```

```python
import functools

import jax
import jax.numpy as jnp
from jax import lax
from jax.experimental import pallas as pl
from jax.experimental.pallas import tpu as pltpu
from jax.sharding import PartitionSpec as P

AXES = ("view", "render")
LZ, NX, NC, HZ = 2, 4, 2, 4
NZ = LZ * HZ
F32 = jnp.float32
BF16 = jnp.bfloat16
STEPS = (2, 1, 3, 0)
GROUPS = ((0, 1), (2, 3))
DELTA_US, SUM_US, OWN_US = 0.0, 10.0, 10.0


def move(array, target):
    pairs = []
    for zl in range(LZ):
        for x in range(NX):
            for core in range(NC):
                for zh in range(HZ):
                    tl, tx, tc, th = target(zl, x, core, zh)
                    pairs.append(
                        (((zl * NX + x) * NC + core) * HZ + zh, ((tl * NX + tx) * NC + tc) * HZ + th)
                    )
    return lax.ppermute(array, AXES, pairs)


def along_x(array, step):
    return move(array, lambda zl, x, c, zh: (zl, (x + step) % NX, c, zh))


def to_owner(array, step):
    return move(array, lambda zl, x, c, zh: (c, (x + step) % NX, zl, zh))


def along_z(array, step):
    def target(zl, x, c, zh):
        z = (zh * LZ + zl + (1 - 2 * c) * step) % NZ
        return z % LZ, x, c, z // LZ

    return move(array, target)


def swap_core(array):
    return move(array, lambda zl, x, c, zh: (zl, x, 1 - c, zh))


def contract(left, right, left_dim, right_dim):
    return lax.dot_general(
        left, right, (((left_dim,), (right_dim,)), ((), ())), preferred_element_type=F32
    )


def cost(us):
    return pl.CostEstimate(flops=1 + int(us * 1.15e9), bytes_accessed=1, transcendentals=0)


def params(mib=32):
    return pltpu.CompilerParams(vmem_limit_bytes=mib * 1024 * 1024)


def delta_kernel(group, place, rates, keys, values, gate, up, down, *refs):
    mine, others, old = refs[: len(GROUPS)], refs[len(GROUPS) : 2 * len(GROUPS)], refs[2 * len(GROUPS)]
    old_turned, k_ref, v_ref, columns, turned, sems = refs[-6:]
    x, zl, core = place[0], place[1], place[2]
    units = gate.shape[2] // NX
    half = units // NC
    n = units * group

    def fetch(m, weight, i):
        start = pl.multiple_of((x + STEPS[i]) % NX * units, units)
        return pltpu.make_async_copy(
            weight.at[0, :, pl.ds(start, units)],
            columns.at[m, :, i * units : (i + 1) * units],
            sems.at[2 + m * NX + i],
        )

    early = keys.shape[0] // 2
    key_copies = [
        pltpu.make_async_copy(keys.at[lo : lo + early], k_ref.at[lo : lo + early], sems.at[3 * NX + 3 + i])
        for i, lo in enumerate((0, early))
    ]
    value_copy = pltpu.make_async_copy(values, v_ref, sems.at[1])
    copies = [[fetch(m, w, i) for i in range(NX)] for m, w in enumerate((gate, up, down))]
    key_copies[0].start()
    for i in range(group):
        copies[0][i].start()
        copies[1][i].start()
    key_copies[1].start()
    value_copy.start()
    for i in range(group):
        copies[2][i].start()
    for i in range(group, NX):
        for m in range(3):
            copies[m][i].start()

    key_copies[0].wait()
    for first in range(0, NX, group):
        blocks = range(first, first + group)
        cut = slice(first * units, first * units + n)
        for i in blocks:
            copies[0][i].wait()
            copies[1][i].wait()
        early_in = [contract(columns[m, :, cut], k_ref[:early], 0, 1) for m in range(2)]
        if not first:
            key_copies[1].wait()
        late_in = [contract(columns[m, :, cut], k_ref[early:], 0, 1) for m in range(2)]
        gate_in, up_in = (jnp.concatenate(pair, 1) for pair in zip(early_in, late_in))
        k = k_ref[...]
        if not first:
            value_copy.wait()
        for i in blocks:
            copies[2][i].wait()
        v, r = v_ref[...], rates[...]
        back = contract(columns[2, :, cut], v, 0, 1)
        s = jax.nn.sigmoid(gate_in)
        act = gate_in * s
        rated = r * back
        turned[0, cut] = (rated * up_in * s * (1.0 + gate_in * (1.0 - s))).astype(BF16)
        turned[1, cut] = (rated * act).astype(BF16)
        turned[2, cut] = (r * (act * up_in)).astype(BF16)
        parts = [(c, i) for c in (1 - core, core) for i in blocks]
        rows = [pl.ds(pl.multiple_of(i * units + c * half, half), half) for c, i in parts]
        pres = jnp.concatenate([turned[m, part] for part in rows for m in (0, 1)], 0)
        key_sums = contract(pres, k, 1, 0).astype(BF16)
        hidden = jnp.concatenate([turned[2, part] for part in rows], 0)
        value_sums = contract(hidden, v, 1, 0).astype(BF16)
        for at, (_, i) in enumerate(parts):
            g = next(g for g in reversed(range(len(GROUPS))) if GROUPS[g][0] <= i)
            out = (mine if at >= group else others)[g].at[i - GROUPS[g][0]]
            out[0] = key_sums[2 * at * half : (2 * at + 1) * half]
            out[1] = key_sums[(2 * at + 1) * half : (2 * at + 2) * half]
            out[2] = value_sums[at * half : (at + 1) * half]
    own = pl.ds(pl.multiple_of(zl * half, half), half)
    for m in range(3):
        old_turned[...] = columns[m, :, (NX - 1) * units :].astype(F32).T
        old[m] = old_turned[own, :].astype(BF16)


def deltas(place, rates, arrays, group=4):
    count, width = arrays[0].shape
    n = arrays[2].shape[2]
    units = n // NX
    half = units // NC
    vmem = pl.BlockSpec(memory_space=pltpu.VMEM)
    out_shape = [jax.ShapeDtypeStruct((len(g), 3, half, width), BF16) for g in GROUPS * 2]
    out_shape.append(jax.ShapeDtypeStruct((3, half, width), BF16))
    return pl.pallas_call(
        functools.partial(delta_kernel, group),
        name="deltas",
        in_specs=[pl.BlockSpec(memory_space=pltpu.SMEM), vmem]
        + [pl.BlockSpec(memory_space=pl.ANY)] * len(arrays),
        out_specs=[vmem] * len(out_shape),
        out_shape=out_shape,
        scratch_shapes=[
            pltpu.VMEM((units, width), F32),
            pltpu.VMEM((count, width), BF16),
            pltpu.VMEM((count, width), BF16),
            pltpu.VMEM((3, width, n), BF16),
            pltpu.VMEM((3, n, count), BF16),
            pltpu.SemaphoreType.DMA((3 * NX + 5,)),
        ],
        compiler_params=params(50),
        cost_estimate=cost(DELTA_US),
    )(place, rates, *arrays)


def call(kernel, name, out_shape, *operands, us=0.0):
    vmem = pl.BlockSpec(memory_space=pltpu.VMEM)
    return pl.pallas_call(
        kernel,
        name=name,
        in_specs=[pl.BlockSpec(memory_space=pltpu.SMEM) if o.ndim == 1 else vmem for o in operands],
        out_specs=jax.tree.map(lambda _: vmem, out_shape),
        out_shape=out_shape,
        compiler_params=params(),
        cost_estimate=cost(us),
    )(*operands)


def add_kernel(mine, other, *outs):
    for i, out in enumerate(outs):
        out[...] = (mine[i].astype(F32) + other[i].astype(F32)).astype(out.dtype)


def add_cores(mine, other):
    block = jax.ShapeDtypeStruct(mine.shape[1:], BF16)
    return call(add_kernel, "add_cores", [block] * mine.shape[0], mine, other)


def sum_kernel(*refs):
    sums = refs[0][...].astype(F32)
    for ref in refs[1:-1]:
        sums = sums + ref[...].astype(F32)
    refs[-1][...] = sums.astype(refs[-1].dtype)


def add_up(name, parts, us):
    return call(sum_kernel, name, jax.ShapeDtypeStruct(parts[0].shape, BF16), *parts, us=us)


def renorm_kernel(place, old, mine, other, *outs):
    n = outs[0].shape[1]
    for m in range(3):
        halves = []
        for i in range(2):
            part = slice(i * n, (i + 1) * n)
            was = old[m, part, :].astype(F32)
            summed = was + (mine[m, part, :].astype(F32) + other[m, part, :].astype(F32))
            factor = jnp.sqrt(jnp.sum(was * was, axis=-1, keepdims=True)) / jnp.sqrt(
                jnp.sum(summed * summed, axis=-1, keepdims=True) + 1e-06
            )
            halves.append((summed * factor).astype(BF16))
        for i, out in enumerate(outs):
            out[m] = jnp.where(place[2] == i, halves[0], halves[1])


def join_kernel(*refs):
    out = refs[-1]
    at = 0
    for ref in refs[:-1]:
        n = ref.shape[1]
        out[:, at : at + n, :] = ref[...]
        at += n


def join(pieces):
    units = sum(p.shape[1] for p in pieces)
    out = jax.ShapeDtypeStruct((3, units, pieces[0].shape[2]), BF16)
    return call(join_kernel, "join", out, *pieces)


def render_kernel(cuts, count, *refs):
    rows, pieces, outs = refs[: len(cuts)], refs[len(cuts) : -count], refs[-count:]
    gate, up, down = (jnp.concatenate([p[m] for p in pieces], 0) for m in range(3))
    q = jnp.concatenate([ref[lo:hi, :] for ref, (lo, hi) in zip(rows, cuts)], 0)
    gate_q = contract(q, gate, 1, 1)
    up_q = contract(q, up, 1, 1)
    hidden_q = (gate_q * jax.nn.sigmoid(gate_q) * up_q).astype(BF16)
    partial = contract(hidden_q, down, 1, 0)
    n = outs[0].shape[0]
    for i, out in enumerate(outs):
        out[...] = partial[i * n : (i + 1) * n].astype(out.dtype)


def render(rows, pieces, outs):
    kernel = functools.partial(render_kernel, tuple((lo, hi) for _, lo, hi in rows), len(outs))
    return call(kernel, "render_rows", outs, *[r[0] for r in rows], *pieces)


def merge_kernel(mid, relay_left, relay_right, to_right, to_left):
    half = to_right.shape[0]
    to_right[...] = (mid[:half] + relay_left[...].astype(F32)).astype(BF16)
    to_left[...] = (mid[half:] + relay_right[...].astype(F32)).astype(BF16)


def own_kernel(own, from_left, from_right, out):
    half = from_left.shape[0]
    out[:half] = own[:half] + from_right[...].astype(F32)
    out[half:] = own[half:] + from_left[...].astype(F32)


def total_kernel(own, last_left, last_right, out):
    half = last_left.shape[0]
    out[:half] = (own[:half] + last_left[...].astype(F32)).astype(BF16)
    out[half:] = (own[half:] + last_right[...].astype(F32)).astype(BF16)


def local(input_keys, input_values, token_rates, gate_weight, up_weight, down_weight, queries):
    view = lax.axis_index("view")
    zl, x, core = view // (NX * NC), (view // NC) % NX, view % NC
    place = jnp.stack([x, zl, core]).astype(jnp.int32)

    arrays = (input_keys, input_values, gate_weight, up_weight, down_weight)
    *parts, old = deltas(place, token_rates, arrays)
    chips = []
    for mine, other in zip(parts, parts[len(GROUPS) :]):
        chips += add_cores(mine, swap_core(other))
    got = [to_owner(chip, step) for chip, step in zip(chips, STEPS)]

    queries, *got[:2] = lax.optimization_barrier((queries, *got[:2]))
    half = queries.shape[0] // 2
    from_right, from_left = along_x(queries, -1), along_x(queries, 1)
    sums = add_up("sum_chips", got, SUM_US)
    out = jax.ShapeDtypeStruct((3, sums.shape[1] // 2, sums.shape[2]), BF16)
    news = call(renorm_kernel, "renorm", [out] * 2, place, old, sums, swap_core(sums))
    first = [along_z(new, 1) for new in news]
    second = [along_z(piece, 1) for piece in first]
    third = [along_z(piece, 1) for piece in second]
    far_top, far_low = along_x(from_right[:half], -1), along_x(from_left[half:], 1)
    third[1], far_top, far_low = lax.optimization_barrier((third[1], far_top, far_low))
    fourth = along_z(third[0], 1)
    near, last = join(first + second), join(third + [fourth])
    pieces = list(news) + [near, swap_core(near), last, swap_core(last)]

    both = 2 * half
    part = jax.ShapeDtypeStruct((half, queries.shape[1]), BF16)
    to_right, to_left = render([(far_top, 0, half), (far_low, 0, half)], pieces, [part] * 2)
    relay_left, relay_right = along_x(to_right, 1), along_x(to_left, -1)
    to_right, to_left = render([(from_right, half, both), (from_left, 0, half)], pieces, [part] * 2)
    from_left_x, from_right_x = along_x(to_right, 1), along_x(to_left, -1)
    wide = jax.ShapeDtypeStruct((both, queries.shape[1]), F32)
    (mid,) = render([(from_right, 0, half), (from_left, half, both)], pieces, [wide])
    (own,) = render([(queries, 0, both)], pieces, [wide])
    to_right, to_left = call(merge_kernel, "merge", [part] * 2, mid, relay_left, relay_right)
    last_left, last_right = along_x(to_right, 1), along_x(to_left, -1)
    own = call(own_kernel, "own", wide, own, from_left_x, from_right_x, us=OWN_US)
    out = jax.ShapeDtypeStruct(own.shape, BF16)
    return call(total_kernel, "total", out, own, last_left, last_right)


def solution(mesh):
    return jax.shard_map(
        local,
        mesh=mesh,
        in_specs=(
            P("view", "head"),
            P("view", "head"),
            P("head", "view"),
            P("head", None, "render"),
            P("head", None, "render"),
            P("head", None, "render"),
            P(("view", "render"), "head"),
        ),
        out_specs=P(("view", "render"), "head"),
        check_vma=False,
    )
```

```python
import functools

import jax
import jax.numpy as jnp
from jax import lax
from jax.experimental import pallas as pl
from jax.experimental.pallas import tpu as pltpu
from jax.sharding import PartitionSpec as P

AXES = ("view", "render")
LZ, NX, NC, HZ = 2, 4, 2, 4
NZ = LZ * HZ
F32 = jnp.float32
BF16 = jnp.bfloat16
STEPS = (2, 1, 3, 0)
GROUPS = ((0, 1), (2, 3))
DELTA_US, SUM_US, OWN_US = 0.0, 10.0, 10.0


def move(array, target):
    pairs = []
    for zl in range(LZ):
        for x in range(NX):
            for core in range(NC):
                for zh in range(HZ):
                    tl, tx, tc, th = target(zl, x, core, zh)
                    pairs.append(
                        (((zl * NX + x) * NC + core) * HZ + zh, ((tl * NX + tx) * NC + tc) * HZ + th)
                    )
    return lax.ppermute(array, AXES, pairs)


def along_x(array, step):
    return move(array, lambda zl, x, c, zh: (zl, (x + step) % NX, c, zh))


def to_owner(array, step):
    return move(array, lambda zl, x, c, zh: (c, (x + step) % NX, zl, zh))


def along_z(array, step):
    def target(zl, x, c, zh):
        z = (zh * LZ + zl + (1 - 2 * c) * step) % NZ
        return z % LZ, x, c, z // LZ

    return move(array, target)


def swap_core(array):
    return move(array, lambda zl, x, c, zh: (zl, x, 1 - c, zh))


def coordinates():
    view = lax.axis_index("view")
    return lax.rem(lax.div(view, NC), NX), lax.div(view, NX * NC), lax.rem(view, NC)


def contract(left, right, left_dim, right_dim):
    return lax.dot_general(
        left, right, (((left_dim,), (right_dim,)), ((), ())), preferred_element_type=F32
    )


def cost(us):
    return pl.CostEstimate(flops=1 + int(us * 1.15e9), bytes_accessed=1, transcendentals=0)


def params(mib=32):
    return pltpu.CompilerParams(vmem_limit_bytes=mib * 1024 * 1024)


def delta_kernel(rates, keys, values, gate, up, down, *refs):
    groups = len(GROUPS)
    mine, other, old = refs[:groups], refs[groups : 2 * groups], refs[2 * groups]
    old_turned, k_ref, v_ref, columns, turned, sems = refs[2 * groups + 1 :]
    x, zl, core = coordinates()
    units = gate.shape[2] // NX
    half = units // NC
    early = keys.shape[0] // 2

    copies = [
        pltpu.make_async_copy(keys.at[:early], k_ref.at[:early], sems.at[0]),
        pltpu.make_async_copy(gate.at[0], columns.at[0], sems.at[1]),
        pltpu.make_async_copy(up.at[0], columns.at[1], sems.at[2]),
        pltpu.make_async_copy(keys.at[early:], k_ref.at[early:], sems.at[3]),
        pltpu.make_async_copy(values, v_ref, sems.at[4]),
        pltpu.make_async_copy(down.at[0], columns.at[2], sems.at[5]),
    ]
    for copy in copies:
        copy.start()
    copies[0].wait()
    parts = []
    for m in range(2):
        copies[1 + m].wait()
        parts.append(contract(columns[m], k_ref[:early], 0, 1))
    copies[3].wait()
    gate_in, up_in = (
        jnp.concatenate([part, contract(columns[m], k_ref[early:], 0, 1)], 1)
        for m, part in enumerate(parts)
    )
    copies[4].wait()
    copies[5].wait()
    k, v, r = k_ref[...], v_ref[...], rates[...]
    back = contract(columns[2], v, 0, 1)
    s = jax.nn.sigmoid(gate_in)
    act = gate_in * s
    rated = r * back
    turned[0] = (rated * up_in * s * (1.0 + gate_in * (1.0 - s))).astype(BF16)
    turned[1] = (rated * act).astype(BF16)
    turned[2] = (r * (act * up_in)).astype(BF16)
    pairs = [(c, i) for c in (1 - core, core) for i in range(NX)]
    rows = [
        pl.ds(pl.multiple_of((x + STEPS[i]) % NX * units + c * half, half), half) for c, i in pairs
    ]
    for m, tokens in enumerate((k, k, v)):
        sums = contract(jnp.concatenate([turned[m, part] for part in rows], 0), tokens, 1, 0).astype(BF16)
        for at, (_, i) in enumerate(pairs):
            g = next(g for g in range(groups) if i in GROUPS[g])
            (mine if at >= NX else other)[g][i - GROUPS[g][0], m] = sums[at * half : (at + 1) * half]
    block = pl.ds(pl.multiple_of(x * units, units), units)
    own = pl.ds(pl.multiple_of(zl * half, half), half)
    for m in range(3):
        old_turned[...] = columns[m, :, block].astype(F32).T
        old[m] = old_turned[own, :].astype(BF16)


def deltas(rates, arrays):
    count, width = arrays[0].shape
    n = arrays[2].shape[2]
    units = n // NX
    half = units // NC
    vmem = pl.BlockSpec(memory_space=pltpu.VMEM)
    out_shape = [jax.ShapeDtypeStruct((len(g), 3, half, width), BF16) for g in GROUPS * 2]
    out_shape.append(jax.ShapeDtypeStruct((3, half, width), BF16))
    return pl.pallas_call(
        delta_kernel,
        name="deltas",
        in_specs=[vmem] + [pl.BlockSpec(memory_space=pl.ANY)] * len(arrays),
        out_specs=[vmem] * len(out_shape),
        out_shape=out_shape,
        scratch_shapes=[
            pltpu.VMEM((units, width), F32),
            pltpu.VMEM((count, width), BF16),
            pltpu.VMEM((count, width), BF16),
            pltpu.VMEM((3, width, n), BF16),
            pltpu.VMEM((3, n, count), BF16),
            pltpu.SemaphoreType.DMA((6,)),
        ],
        compiler_params=params(50),
        cost_estimate=cost(DELTA_US),
    )(rates, *arrays)


def call(kernel, name, out_shape, *operands, us=0.0):
    vmem = pl.BlockSpec(memory_space=pltpu.VMEM)
    return pl.pallas_call(
        kernel,
        name=name,
        in_specs=[vmem] * len(operands),
        out_specs=jax.tree.map(lambda _: vmem, out_shape),
        out_shape=out_shape,
        compiler_params=params(),
        cost_estimate=cost(us),
    )(*operands)


def add_kernel(mine, other, *outs):
    for i, out in enumerate(outs):
        out[...] = (mine[i].astype(F32) + other[i].astype(F32)).astype(out.dtype)


def add_cores(mine, other):
    block = jax.ShapeDtypeStruct(mine.shape[1:], BF16)
    return call(add_kernel, "add_cores", [block] * mine.shape[0], mine, other)


def sum_kernel(*refs):
    sums = refs[0][...].astype(F32)
    for ref in refs[1:-1]:
        sums = sums + ref[...].astype(F32)
    refs[-1][...] = sums.astype(refs[-1].dtype)


def add_up(name, parts, us):
    return call(sum_kernel, name, jax.ShapeDtypeStruct(parts[0].shape, BF16), *parts, us=us)


def renorm_kernel(old, mine, other, *outs):
    n = outs[0].shape[1]
    _, _, core = coordinates()
    for m in range(3):
        halves = []
        for i in range(2):
            part = slice(i * n, (i + 1) * n)
            was = old[m, part, :].astype(F32)
            summed = was + (mine[m, part, :].astype(F32) + other[m, part, :].astype(F32))
            factor = jnp.sqrt(jnp.sum(was * was, axis=-1, keepdims=True)) / jnp.sqrt(
                jnp.sum(summed * summed, axis=-1, keepdims=True) + 1e-06
            )
            halves.append(summed * factor)
        for i, out in enumerate(outs):
            out[m] = jnp.where(core == i, halves[0], halves[1]).astype(BF16)


def join_kernel(*refs):
    out = refs[-1]
    at = 0
    for ref in refs[:-1]:
        n = ref.shape[1]
        out[:, at : at + n, :] = ref[...]
        at += n


def join(pieces):
    units = sum(p.shape[1] for p in pieces)
    out = jax.ShapeDtypeStruct((3, units, pieces[0].shape[2]), BF16)
    return call(join_kernel, "join", out, *pieces)


def render_kernel(cuts, count, added, *refs):
    rows, pieces, outs = refs[: len(cuts)], refs[len(cuts) : -count], refs[-count:]
    if added:
        *pieces, before = pieces
    gate, up, down = (jnp.concatenate([p[m] for p in pieces], 0) for m in range(3))
    q = jnp.concatenate([ref[lo:hi, :] for ref, (lo, hi) in zip(rows, cuts)], 0)
    gate_q = contract(q, gate, 1, 1)
    up_q = contract(q, up, 1, 1)
    hidden_q = (gate_q * jax.nn.sigmoid(gate_q) * up_q).astype(BF16)
    partial = contract(hidden_q, down, 1, 0)
    if added:
        partial = before[...] + partial
    n = outs[0].shape[0]
    for i, out in enumerate(outs):
        out[...] = partial[i * n : (i + 1) * n].astype(out.dtype)


def render(rows, pieces, outs, before=None):
    cuts = tuple((lo, hi) for _, lo, hi in rows)
    kernel = functools.partial(render_kernel, cuts, len(outs), before is not None)
    operands = [r[0] for r in rows] + list(pieces) + ([] if before is None else [before])
    return call(kernel, "render_rows", outs, *operands)


def merge_kernel(mid, relay_left, relay_right, to_right, to_left):
    half = to_right.shape[0]
    to_right[...] = (mid[:half] + relay_left[...].astype(F32)).astype(BF16)
    to_left[...] = (mid[half:] + relay_right[...].astype(F32)).astype(BF16)


def own_kernel(own, from_left, from_right, out):
    half = from_left.shape[0]
    out[:half] = own[:half] + from_right[...].astype(F32)
    out[half:] = own[half:] + from_left[...].astype(F32)


def total_kernel(own, last_left, last_right, out):
    half = last_left.shape[0]
    out[:half] = (own[:half] + last_left[...].astype(F32)).astype(BF16)
    out[half:] = (own[half:] + last_right[...].astype(F32)).astype(BF16)


def local(input_keys, input_values, token_rates, gate_weight, up_weight, down_weight, queries):
    arrays = (input_keys, input_values, gate_weight, up_weight, down_weight)
    *parts, old = deltas(token_rates, arrays)
    chips = []
    for mine, other in zip(parts, parts[len(GROUPS) :]):
        chips += add_cores(mine, swap_core(other))
    got = [to_owner(chip, step) for chip, step in zip(chips, STEPS)]

    queries, *got[:2] = lax.optimization_barrier((queries, *got[:2]))
    half = queries.shape[0] // 2
    from_right, from_left = along_x(queries, -1), along_x(queries, 1)
    sums = add_up("sum_chips", got, SUM_US)
    out = jax.ShapeDtypeStruct((3, sums.shape[1] // 2, sums.shape[2]), BF16)
    news = call(renorm_kernel, "renorm", [out] * 2, old, sums, swap_core(sums))
    first = [along_z(new, 1) for new in news]
    second = [along_z(piece, 1) for piece in first]
    third = [along_z(piece, 1) for piece in second]
    far_top, far_low = along_x(from_right[:half], -1), along_x(from_left[half:], 1)
    third[1], far_top, far_low = lax.optimization_barrier((third[1], far_top, far_low))
    fourth = along_z(third[0], 1)
    near, last = join(first + second), join(third + [fourth])
    early, late = list(news) + [near, last], [swap_core(near), swap_core(last)]

    both, width = 2 * half, queries.shape[1]
    part = jax.ShapeDtypeStruct((half, width), BF16)
    wide = jax.ShapeDtypeStruct((both, width), F32)
    sets = [
        ([(far_top, 0, half), (far_low, 0, half)], [part] * 2),
        ([(from_right, half, both), (from_left, 0, half)], [part] * 2),
        ([(from_right, 0, half), (from_left, half, both)], [wide]),
        ([(queries, 0, both)], [wide]),
    ]
    (before,) = render(sets[0][0], early, [wide])
    late[1], before = lax.optimization_barrier((late[1], before))
    to_right, to_left = render(sets[0][0], late, sets[0][1], before)
    direct, (mid,), (own,) = (render(rows, early + late, outs) for rows, outs in sets[1:])
    relay_left, relay_right = along_x(to_right, 1), along_x(to_left, -1)
    from_left_x, from_right_x = along_x(direct[0], 1), along_x(direct[1], -1)
    to_right, to_left = call(merge_kernel, "merge", [part] * 2, mid, relay_left, relay_right)
    last_left, last_right = along_x(to_right, 1), along_x(to_left, -1)
    own = call(own_kernel, "own", wide, own, from_left_x, from_right_x, us=OWN_US)
    out = jax.ShapeDtypeStruct(own.shape, BF16)
    return call(total_kernel, "total", out, own, last_left, last_right)


def solution(mesh):
    return jax.shard_map(
        local,
        mesh=mesh,
        in_specs=(
            P("view", "head"),
            P("view", "head"),
            P("head", "view"),
            P("head", None, "render"),
            P("head", None, "render"),
            P("head", None, "render"),
            P(("view", "render"), "head"),
        ),
        out_specs=P(("view", "render"), "head"),
        check_vma=False,
    )
```

```python
import functools

import jax
import jax.numpy as jnp
from jax import lax
from jax.experimental import pallas as pl
from jax.experimental.pallas import tpu as pltpu
from jax.sharding import PartitionSpec as P

AXES = ("view", "render")
LZ, NX, NC, HZ = 2, 4, 2, 4
NZ = LZ * HZ
F32 = jnp.float32
BF16 = jnp.bfloat16
STEPS = (1, 3, 2, 0)
GROUPS = ((0,), (1,), (2,), (3,))
DELTA_US, SUM_US, OWN_US = 0.0, 10.0, 10.0


def move(array, target):
    pairs = []
    for zl in range(LZ):
        for x in range(NX):
            for core in range(NC):
                for zh in range(HZ):
                    tl, tx, tc, th = target(zl, x, core, zh)
                    pairs.append(
                        (((zl * NX + x) * NC + core) * HZ + zh, ((tl * NX + tx) * NC + tc) * HZ + th)
                    )
    return lax.ppermute(array, AXES, pairs)


def along_x(array, step):
    return move(array, lambda zl, x, c, zh: (zl, (x + step) % NX, c, zh))


def to_owner(array, step):
    return move(array, lambda zl, x, c, zh: (c, (x + step) % NX, zl, zh))


def along_z(array, step):
    def target(zl, x, c, zh):
        z = (zh * LZ + zl + (1 - 2 * c) * step) % NZ
        return z % LZ, x, c, z // LZ

    return move(array, target)


def swap_core(array):
    return move(array, lambda zl, x, c, zh: (zl, x, 1 - c, zh))


def coordinates():
    view = lax.axis_index("view")
    return lax.rem(lax.div(view, NC), NX), lax.div(view, NX * NC), lax.rem(view, NC)


def contract(left, right, left_dim, right_dim):
    return lax.dot_general(
        left, right, (((left_dim,), (right_dim,)), ((), ())), preferred_element_type=F32
    )


def cost(us):
    return pl.CostEstimate(flops=1 + int(us * 1.15e9), bytes_accessed=1, transcendentals=0)


def params(mib=32):
    return pltpu.CompilerParams(vmem_limit_bytes=mib * 1024 * 1024)


def delta_kernel(rates, keys, values, gate, up, down, *refs):
    groups = len(GROUPS)
    mine, other, old = refs[:groups], refs[groups : 2 * groups], refs[2 * groups]
    r_ref, old_turned, k_ref, v_ref, columns, turned, sems = refs[2 * groups + 1 :]
    x, zl, core = coordinates()
    units = gate.shape[2] // NX
    half = units // NC
    early = keys.shape[0] // 2

    copies = [
        pltpu.make_async_copy(keys.at[:early], k_ref.at[:early], sems.at[0]),
        pltpu.make_async_copy(gate.at[0], columns.at[0], sems.at[1]),
        pltpu.make_async_copy(up.at[0], columns.at[1], sems.at[2]),
        pltpu.make_async_copy(keys.at[early:], k_ref.at[early:], sems.at[3]),
        pltpu.make_async_copy(values, v_ref, sems.at[4]),
        pltpu.make_async_copy(down.at[0], columns.at[2], sems.at[5]),
        pltpu.make_async_copy(rates, r_ref, sems.at[6]),
    ]
    for copy in copies:
        copy.start()
    copies[0].wait()
    parts = []
    for m in range(2):
        copies[1 + m].wait()
        parts.append(contract(columns[m], k_ref[:early], 0, 1))
    copies[3].wait()
    gate_in, up_in = (
        jnp.concatenate([part, contract(columns[m], k_ref[early:], 0, 1)], 1)
        for m, part in enumerate(parts)
    )
    copies[4].wait()
    copies[5].wait()
    copies[6].wait()
    k, v, r = k_ref[...], v_ref[...], r_ref[...]
    back = contract(columns[2], v, 0, 1)
    s = jax.nn.sigmoid(gate_in)
    act = gate_in * s
    rated = r * back
    turned[0] = (rated * up_in * s * (1.0 + gate_in * (1.0 - s))).astype(BF16)
    turned[1] = (rated * act).astype(BF16)
    turned[2] = (r * (act * up_in)).astype(BF16)
    pairs = [(c, i) for c in (1 - core, core) for i in range(NX)]
    rows = [
        pl.ds(pl.multiple_of((x + STEPS[i]) % NX * units + c * half, half), half) for c, i in pairs
    ]
    for m, tokens in enumerate((k, k, v)):
        sums = contract(jnp.concatenate([turned[m, part] for part in rows], 0), tokens, 1, 0).astype(BF16)
        for at, (_, i) in enumerate(pairs):
            g = next(g for g in range(groups) if i in GROUPS[g])
            (mine if at >= NX else other)[g][i - GROUPS[g][0], m] = sums[at * half : (at + 1) * half]
    block = pl.ds(pl.multiple_of(x * units, units), units)
    own = pl.ds(pl.multiple_of(zl * half, half), half)
    for m in range(3):
        old_turned[...] = columns[m, :, block].astype(F32).T
        old[m] = old_turned[own, :].astype(BF16)


def deltas(rates, arrays):
    count, width = arrays[0].shape
    n = arrays[2].shape[2]
    units = n // NX
    half = units // NC
    vmem = pl.BlockSpec(memory_space=pltpu.VMEM)
    out_shape = [jax.ShapeDtypeStruct((len(g), 3, half, width), BF16) for g in GROUPS * 2]
    out_shape.append(jax.ShapeDtypeStruct((3, half, width), BF16))
    return pl.pallas_call(
        delta_kernel,
        name="deltas",
        in_specs=[pl.BlockSpec(memory_space=pltpu.HBM)] + [pl.BlockSpec(memory_space=pl.ANY)] * len(arrays),
        out_specs=[vmem] * len(out_shape),
        out_shape=out_shape,
        scratch_shapes=[
            pltpu.VMEM((1, count), F32),
            pltpu.VMEM((units, width), F32),
            pltpu.VMEM((count, width), BF16),
            pltpu.VMEM((count, width), BF16),
            pltpu.VMEM((3, width, n), BF16),
            pltpu.VMEM((3, n, count), BF16),
            pltpu.SemaphoreType.DMA((7,)),
        ],
        compiler_params=params(50),
        cost_estimate=cost(DELTA_US),
    )(rates, *arrays)


def call(kernel, name, out_shape, *operands, us=0.0):
    vmem = pl.BlockSpec(memory_space=pltpu.VMEM)
    return pl.pallas_call(
        kernel,
        name=name,
        in_specs=[vmem] * len(operands),
        out_specs=jax.tree.map(lambda _: vmem, out_shape),
        out_shape=out_shape,
        compiler_params=params(),
        cost_estimate=cost(us),
    )(*operands)


def add_kernel(mine, other, *outs):
    for i, out in enumerate(outs):
        out[...] = (mine[i].astype(F32) + other[i].astype(F32)).astype(out.dtype)


def add_cores(mine, other):
    block = jax.ShapeDtypeStruct(mine.shape[1:], BF16)
    return call(add_kernel, "add_cores", [block] * mine.shape[0], mine, other)


def sum_kernel(*refs):
    sums = refs[0][...].astype(F32)
    for ref in refs[1:-1]:
        sums = sums + ref[...].astype(F32)
    refs[-1][...] = sums.astype(refs[-1].dtype)


def add_up(name, parts, us):
    return call(sum_kernel, name, jax.ShapeDtypeStruct(parts[0].shape, BF16), *parts, us=us)


def renorm_kernel(old, mine, other, *outs):
    n = outs[0].shape[1]
    _, _, core = coordinates()
    for m in range(3):
        halves = []
        for i in range(2):
            part = slice(i * n, (i + 1) * n)
            was = old[m, part, :].astype(F32)
            summed = was + (mine[m, part, :].astype(F32) + other[m, part, :].astype(F32))
            factor = jnp.sqrt(jnp.sum(was * was, axis=-1, keepdims=True)) / jnp.sqrt(
                jnp.sum(summed * summed, axis=-1, keepdims=True) + 1e-06
            )
            halves.append(summed * factor)
        for i, out in enumerate(outs):
            out[m] = jnp.where(core == i, halves[0], halves[1]).astype(BF16)


def join_kernel(*refs):
    out = refs[-1]
    at = 0
    for ref in refs[:-1]:
        n = ref.shape[1]
        out[:, at : at + n, :] = ref[...]
        at += n


def join(pieces):
    units = sum(p.shape[1] for p in pieces)
    out = jax.ShapeDtypeStruct((3, units, pieces[0].shape[2]), BF16)
    return call(join_kernel, "join", out, *pieces)


def render_kernel(cuts, count, added, *refs):
    rows, pieces, outs = refs[: len(cuts)], refs[len(cuts) : -count], refs[-count:]
    if added:
        *pieces, before = pieces
    gate, up, down = (jnp.concatenate([p[m] for p in pieces], 0) for m in range(3))
    q = jnp.concatenate([ref[lo:hi, :] for ref, (lo, hi) in zip(rows, cuts)], 0)
    gate_q = contract(q, gate, 1, 1)
    up_q = contract(q, up, 1, 1)
    hidden_q = (gate_q * jax.nn.sigmoid(gate_q) * up_q).astype(BF16)
    partial = contract(hidden_q, down, 1, 0)
    if added:
        partial = before[...] + partial
    n = outs[0].shape[0]
    for i, out in enumerate(outs):
        out[...] = partial[i * n : (i + 1) * n].astype(out.dtype)


def render(rows, pieces, outs, before=None):
    cuts = tuple((lo, hi) for _, lo, hi in rows)
    kernel = functools.partial(render_kernel, cuts, len(outs), before is not None)
    operands = [r[0] for r in rows] + list(pieces) + ([] if before is None else [before])
    return call(kernel, "render_rows", outs, *operands)


def merge_kernel(mid, relay_left, relay_right, to_right, to_left):
    half = to_right.shape[0]
    to_right[...] = (mid[:half] + relay_left[...].astype(F32)).astype(BF16)
    to_left[...] = (mid[half:] + relay_right[...].astype(F32)).astype(BF16)


def own_kernel(own, from_left, from_right, out):
    half = from_left.shape[0]
    out[:half] = own[:half] + from_right[...].astype(F32)
    out[half:] = own[half:] + from_left[...].astype(F32)


def total_kernel(own, last_left, last_right, out):
    half = last_left.shape[0]
    out[:half] = (own[:half] + last_left[...].astype(F32)).astype(BF16)
    out[half:] = (own[half:] + last_right[...].astype(F32)).astype(BF16)


def local(input_keys, input_values, token_rates, gate_weight, up_weight, down_weight, queries):
    arrays = (input_keys, input_values, gate_weight, up_weight, down_weight)
    rates = pltpu.with_memory_space_constraint(token_rates, pltpu.HBM)
    *parts, old = deltas(rates, arrays)
    chips = []
    for mine, other in zip(parts, parts[len(GROUPS) :]):
        chips += add_cores(mine, swap_core(other))
    got = [to_owner(chip, step) for chip, step in zip(chips, STEPS)]

    queries, *got[:2] = lax.optimization_barrier((queries, *got[:2]))
    half = queries.shape[0] // 2
    from_right, from_left = along_x(queries, -1), along_x(queries, 1)
    sums = add_up("sum_chips", got, SUM_US)
    out = jax.ShapeDtypeStruct((3, sums.shape[1] // 2, sums.shape[2]), BF16)
    news = call(renorm_kernel, "renorm", [out] * 2, old, sums, swap_core(sums))
    first = [along_z(new, 1) for new in news]
    second = [along_z(piece, 1) for piece in first]
    third = [along_z(piece, 1) for piece in second]
    far_top, far_low = along_x(from_right[:half], -1), along_x(from_left[half:], 1)
    third[1], far_top, far_low = lax.optimization_barrier((third[1], far_top, far_low))
    fourth = along_z(third[0], 1)
    near, last = join(first + second), join(third + [fourth])
    early, late = list(news) + [near, last], [swap_core(near), swap_core(last)]

    both, width = 2 * half, queries.shape[1]
    part = jax.ShapeDtypeStruct((half, width), BF16)
    wide = jax.ShapeDtypeStruct((both, width), F32)
    sets = [
        ([(far_top, 0, half), (far_low, 0, half)], [part] * 2),
        ([(from_right, half, both), (from_left, 0, half)], [part] * 2),
        ([(from_right, 0, half), (from_left, half, both)], [wide]),
        ([(queries, 0, both)], [wide]),
    ]
    (before,) = render(sets[0][0], early, [wide])
    late[1], before = lax.optimization_barrier((late[1], before))
    to_right, to_left = render(sets[0][0], late, sets[0][1], before)
    direct, (mid,), (own,) = (render(rows, early + late, outs) for rows, outs in sets[1:])
    relay_left, relay_right = along_x(to_right, 1), along_x(to_left, -1)
    from_left_x, from_right_x = along_x(direct[0], 1), along_x(direct[1], -1)
    to_right, to_left = call(merge_kernel, "merge", [part] * 2, mid, relay_left, relay_right)
    last_left, last_right = along_x(to_right, 1), along_x(to_left, -1)
    own = call(own_kernel, "own", wide, own, from_left_x, from_right_x, us=OWN_US)
    out = jax.ShapeDtypeStruct(own.shape, BF16)
    return call(total_kernel, "total", out, own, last_left, last_right)


def solution(mesh):
    return jax.shard_map(
        local,
        mesh=mesh,
        in_specs=(
            P("view", "head"),
            P("view", "head"),
            P("head", "view"),
            P("head", None, "render"),
            P("head", None, "render"),
            P("head", None, "render"),
            P(("view", "render"), "head"),
        ),
        out_specs=P(("view", "render"), "head"),
        check_vma=False,
    )
```

```python
import functools

import jax
import jax.numpy as jnp
from jax import lax
from jax.experimental import pallas as pl
from jax.experimental.pallas import tpu as pltpu
from jax.sharding import PartitionSpec as P

AXES = ("view", "render")
LZ, NX, NC, HZ = 2, 4, 2, 4
NZ = LZ * HZ
F32 = jnp.float32
BF16 = jnp.bfloat16
STEPS = (1, 3, 2, 0)
GROUPS = ((0,), (1,), (2,), (3,))
DELTA_US, SUM_US, OWN_US = 0.0, 10.0, 10.0


def move(array, target):
    pairs = []
    for zl in range(LZ):
        for x in range(NX):
            for core in range(NC):
                for zh in range(HZ):
                    tl, tx, tc, th = target(zl, x, core, zh)
                    pairs.append(
                        (((zl * NX + x) * NC + core) * HZ + zh, ((tl * NX + tx) * NC + tc) * HZ + th)
                    )
    return lax.ppermute(array, AXES, pairs)


def along_x(array, step):
    return move(array, lambda zl, x, c, zh: (zl, (x + step) % NX, c, zh))


def to_owner(array, step):
    return move(array, lambda zl, x, c, zh: (c, (x + step) % NX, zl, zh))


def along_z(array, step):
    def target(zl, x, c, zh):
        z = (zh * LZ + zl + (1 - 2 * c) * step) % NZ
        return z % LZ, x, c, z // LZ

    return move(array, target)


def swap_core(array):
    return move(array, lambda zl, x, c, zh: (zl, x, 1 - c, zh))


def coordinates():
    view = lax.axis_index("view")
    return lax.rem(lax.div(view, NC), NX), lax.div(view, NX * NC), lax.rem(view, NC)


def contract(left, right, left_dim, right_dim):
    return lax.dot_general(
        left, right, (((left_dim,), (right_dim,)), ((), ())), preferred_element_type=F32
    )


def cost(us):
    return pl.CostEstimate(flops=1 + int(us * 1.15e9), bytes_accessed=1, transcendentals=0)


def params(mib=32):
    return pltpu.CompilerParams(vmem_limit_bytes=mib * 1024 * 1024)


def delta_kernel(rates, keys, values, gate, up, down, *refs):
    groups = len(GROUPS)
    mine, other, old = refs[:groups], refs[groups : 2 * groups], refs[2 * groups]
    r_ref, old_turned, k_ref, v_ref, columns, turned, sems = refs[2 * groups + 1 :]
    x, zl, core = coordinates()
    units = gate.shape[2] // NX
    half = units // NC
    early = keys.shape[0] // 2

    copies = [
        pltpu.make_async_copy(keys.at[:early], k_ref.at[:early], sems.at[0]),
        pltpu.make_async_copy(gate.at[0], columns.at[0], sems.at[1]),
        pltpu.make_async_copy(up.at[0], columns.at[1], sems.at[2]),
        pltpu.make_async_copy(keys.at[early:], k_ref.at[early:], sems.at[3]),
        pltpu.make_async_copy(values, v_ref, sems.at[4]),
        pltpu.make_async_copy(down.at[0], columns.at[2], sems.at[5]),
        pltpu.make_async_copy(rates, r_ref, sems.at[6]),
    ]
    for copy in copies[:3]:
        copy.start()
    copies[0].wait()
    copies[1].wait()
    for copy in copies[3:]:
        copy.start()
    parts = [contract(columns[0], k_ref[:early], 0, 1)]
    copies[2].wait()
    parts.append(contract(columns[1], k_ref[:early], 0, 1))
    copies[3].wait()
    gate_in, up_in = (
        jnp.concatenate([part, contract(columns[m], k_ref[early:], 0, 1)], 1)
        for m, part in enumerate(parts)
    )
    copies[4].wait()
    copies[5].wait()
    copies[6].wait()
    k, v, r = k_ref[...], v_ref[...], r_ref[...]
    back = contract(columns[2], v, 0, 1)
    s = jax.nn.sigmoid(gate_in)
    act = gate_in * s
    rated = r * back
    turned[0] = (rated * up_in * s * (1.0 + gate_in * (1.0 - s))).astype(BF16)
    turned[1] = (rated * act).astype(BF16)
    turned[2] = (r * (act * up_in)).astype(BF16)
    pairs = [(c, i) for c in (1 - core, core) for i in range(NX)]
    rows = [
        pl.ds(pl.multiple_of((x + STEPS[i]) % NX * units + c * half, half), half) for c, i in pairs
    ]
    for m, tokens in enumerate((k, k, v)):
        sums = contract(jnp.concatenate([turned[m, part] for part in rows], 0), tokens, 1, 0).astype(BF16)
        for at, (_, i) in enumerate(pairs):
            g = next(g for g in range(groups) if i in GROUPS[g])
            (mine if at >= NX else other)[g][i - GROUPS[g][0], m] = sums[at * half : (at + 1) * half]
    block = pl.ds(pl.multiple_of(x * units, units), units)
    own = pl.ds(pl.multiple_of(zl * half, half), half)
    for m in range(3):
        old_turned[...] = columns[m, :, block].astype(F32).T
        old[m] = old_turned[own, :].astype(BF16)


def deltas(rates, arrays):
    count, width = arrays[0].shape
    n = arrays[2].shape[2]
    units = n // NX
    half = units // NC
    vmem = pl.BlockSpec(memory_space=pltpu.VMEM)
    out_shape = [jax.ShapeDtypeStruct((len(g), 3, half, width), BF16) for g in GROUPS * 2]
    out_shape.append(jax.ShapeDtypeStruct((3, half, width), BF16))
    return pl.pallas_call(
        delta_kernel,
        name="deltas",
        in_specs=[pl.BlockSpec(memory_space=pltpu.HBM)] + [pl.BlockSpec(memory_space=pl.ANY)] * len(arrays),
        out_specs=[vmem] * len(out_shape),
        out_shape=out_shape,
        scratch_shapes=[
            pltpu.VMEM((1, count), F32),
            pltpu.VMEM((units, width), F32),
            pltpu.VMEM((count, width), BF16),
            pltpu.VMEM((count, width), BF16),
            pltpu.VMEM((3, width, n), BF16),
            pltpu.VMEM((3, n, count), BF16),
            pltpu.SemaphoreType.DMA((7,)),
        ],
        compiler_params=params(50),
        cost_estimate=cost(DELTA_US),
    )(rates, *arrays)


def call(kernel, name, out_shape, *operands, us=0.0):
    vmem = pl.BlockSpec(memory_space=pltpu.VMEM)
    return pl.pallas_call(
        kernel,
        name=name,
        in_specs=[vmem] * len(operands),
        out_specs=jax.tree.map(lambda _: vmem, out_shape),
        out_shape=out_shape,
        compiler_params=params(),
        cost_estimate=cost(us),
    )(*operands)


def add_kernel(mine, other, *outs):
    for i, out in enumerate(outs):
        out[...] = (mine[i].astype(F32) + other[i].astype(F32)).astype(out.dtype)


def add_cores(mine, other):
    block = jax.ShapeDtypeStruct(mine.shape[1:], BF16)
    return call(add_kernel, "add_cores", [block] * mine.shape[0], mine, other)


def sum_kernel(*refs):
    sums = refs[0][...].astype(F32)
    for ref in refs[1:-1]:
        sums = sums + ref[...].astype(F32)
    refs[-1][...] = sums.astype(refs[-1].dtype)


def add_up(name, parts, us):
    return call(sum_kernel, name, jax.ShapeDtypeStruct(parts[0].shape, BF16), *parts, us=us)


def renorm_kernel(old, mine, other, *outs):
    n = outs[0].shape[1]
    _, _, core = coordinates()
    for m in range(3):
        halves = []
        for i in range(2):
            part = slice(i * n, (i + 1) * n)
            was = old[m, part, :].astype(F32)
            summed = was + (mine[m, part, :].astype(F32) + other[m, part, :].astype(F32))
            factor = jnp.sqrt(jnp.sum(was * was, axis=-1, keepdims=True)) / jnp.sqrt(
                jnp.sum(summed * summed, axis=-1, keepdims=True) + 1e-06
            )
            halves.append(summed * factor)
        for i, out in enumerate(outs):
            out[m] = jnp.where(core == i, halves[0], halves[1]).astype(BF16)


def join_kernel(*refs):
    out = refs[-1]
    at = 0
    for ref in refs[:-1]:
        n = ref.shape[1]
        out[:, at : at + n, :] = ref[...]
        at += n


def join(pieces):
    units = sum(p.shape[1] for p in pieces)
    out = jax.ShapeDtypeStruct((3, units, pieces[0].shape[2]), BF16)
    return call(join_kernel, "join", out, *pieces)


def render_kernel(cuts, count, added, *refs):
    rows, pieces, outs = refs[: len(cuts)], refs[len(cuts) : -count], refs[-count:]
    if added:
        *pieces, before = pieces
    gate, up, down = (jnp.concatenate([p[m] for p in pieces], 0) for m in range(3))
    q = jnp.concatenate([ref[lo:hi, :] for ref, (lo, hi) in zip(rows, cuts)], 0)
    gate_q = contract(q, gate, 1, 1)
    up_q = contract(q, up, 1, 1)
    hidden_q = (gate_q * jax.nn.sigmoid(gate_q) * up_q).astype(BF16)
    partial = contract(hidden_q, down, 1, 0)
    if added:
        partial = before[...] + partial
    n = outs[0].shape[0]
    for i, out in enumerate(outs):
        out[...] = partial[i * n : (i + 1) * n].astype(out.dtype)


def render(rows, pieces, outs, before=None):
    cuts = tuple((lo, hi) for _, lo, hi in rows)
    kernel = functools.partial(render_kernel, cuts, len(outs), before is not None)
    operands = [r[0] for r in rows] + list(pieces) + ([] if before is None else [before])
    return call(kernel, "render_rows", outs, *operands)


def merge_kernel(start, mid, relay, out):
    out[...] = (mid[start : start + out.shape[0]] + relay[...].astype(F32)).astype(BF16)


def own_kernel(own, from_left, from_right, out):
    half = from_left.shape[0]
    out[:half] = own[:half] + from_right[...].astype(F32)
    out[half:] = own[half:] + from_left[...].astype(F32)


def total_kernel(own, last_left, last_right, out):
    half = last_left.shape[0]
    out[:half] = (own[:half] + last_left[...].astype(F32)).astype(BF16)
    out[half:] = (own[half:] + last_right[...].astype(F32)).astype(BF16)


def local(input_keys, input_values, token_rates, gate_weight, up_weight, down_weight, queries):
    arrays = (input_keys, input_values, gate_weight, up_weight, down_weight)
    rates = pltpu.with_memory_space_constraint(token_rates, pltpu.HBM)
    *parts, old = deltas(rates, arrays)
    chips = []
    for mine, other in zip(parts, parts[len(GROUPS) :]):
        chips += add_cores(mine, swap_core(other))
    got = [to_owner(chip, step) for chip, step in zip(chips, STEPS)]

    queries, *got[:2] = lax.optimization_barrier((queries, *got[:2]))
    half = queries.shape[0] // 2
    from_right, from_left = along_x(queries, -1), along_x(queries, 1)
    sums = add_up("sum_chips", got, SUM_US)
    out = jax.ShapeDtypeStruct((3, sums.shape[1] // 2, sums.shape[2]), BF16)
    news = call(renorm_kernel, "renorm", [out] * 2, old, sums, swap_core(sums))
    first = [along_z(new, 1) for new in news]
    second = [along_z(piece, 1) for piece in first]
    third = [along_z(piece, 1) for piece in second]
    far_top, far_low = along_x(from_right[:half], -1), along_x(from_left[half:], 1)
    third[1], far_top, far_low = lax.optimization_barrier((third[1], far_top, far_low))
    fourth = along_z(third[0], 1)
    near, last = join(first + second), join(third + [fourth])
    early, late = list(news) + [near, last], [swap_core(near), swap_core(last)]

    both, width = 2 * half, queries.shape[1]
    part = jax.ShapeDtypeStruct((half, width), BF16)
    wide = jax.ShapeDtypeStruct((both, width), F32)
    sets = [
        ([(far_top, 0, half), (far_low, 0, half)], [part] * 2),
        ([(from_right, half, both), (from_left, 0, half)], [part] * 2),
        ([(from_right, 0, half), (from_left, half, both)], [wide]),
        ([(queries, 0, both)], [wide]),
    ]
    (before,) = render(sets[0][0], early, [wide])
    late[1], before = lax.optimization_barrier((late[1], before))
    to_right, to_left = render(sets[0][0], late, sets[0][1], before)
    direct, (mid,), (own,) = (render(rows, early + late, outs) for rows, outs in sets[1:])
    relay_left, relay_right = along_x(to_right, 1), along_x(to_left, -1)
    from_left_x, from_right_x = along_x(direct[0], 1), along_x(direct[1], -1)
    to_right = call(functools.partial(merge_kernel, 0), "merge", part, mid, relay_left)
    to_left = call(functools.partial(merge_kernel, half), "merge", part, mid, relay_right)
    last_left, last_right = along_x(to_right, 1), along_x(to_left, -1)
    own = call(own_kernel, "own", wide, own, from_left_x, from_right_x, us=OWN_US)
    out = jax.ShapeDtypeStruct(own.shape, BF16)
    return call(total_kernel, "total", out, own, last_left, last_right)


def solution(mesh):
    return jax.shard_map(
        local,
        mesh=mesh,
        in_specs=(
            P("view", "head"),
            P("view", "head"),
            P("head", "view"),
            P("head", None, "render"),
            P("head", None, "render"),
            P("head", None, "render"),
            P(("view", "render"), "head"),
        ),
        out_specs=P(("view", "render"), "head"),
        check_vma=False,
    )
```

```python
import functools

import jax
import jax.numpy as jnp
from jax import lax
from jax.experimental import pallas as pl
from jax.experimental.pallas import tpu as pltpu
from jax.sharding import PartitionSpec as P

AXES = ("view", "render")
LZ, NX, NC, HZ = 2, 4, 2, 4
NZ = LZ * HZ
F32 = jnp.float32
BF16 = jnp.bfloat16
STEPS = (3, 1, 2, 0)
GROUPS = ((0,), (1,), (2,), (3,))
DELTA_US, SUM_US, OWN_US = 0.0, 10.0, 10.0


def move(array, target):
    pairs = []
    for zl in range(LZ):
        for x in range(NX):
            for core in range(NC):
                for zh in range(HZ):
                    tl, tx, tc, th = target(zl, x, core, zh)
                    pairs.append(
                        (((zl * NX + x) * NC + core) * HZ + zh, ((tl * NX + tx) * NC + tc) * HZ + th)
                    )
    return lax.ppermute(array, AXES, pairs)


def along_x(array, step):
    return move(array, lambda zl, x, c, zh: (zl, (x + step) % NX, c, zh))


def to_owner(array, step):
    return move(array, lambda zl, x, c, zh: (c, (x + step) % NX, zl, zh))


def along_z(array, step):
    def target(zl, x, c, zh):
        z = (zh * LZ + zl + (1 - 2 * c) * step) % NZ
        return z % LZ, x, c, z // LZ

    return move(array, target)


def swap_core(array):
    return move(array, lambda zl, x, c, zh: (zl, x, 1 - c, zh))


def coordinates():
    view = lax.axis_index("view")
    return lax.rem(lax.div(view, NC), NX), lax.div(view, NX * NC), lax.rem(view, NC)


def contract(left, right, left_dim, right_dim):
    return lax.dot_general(
        left, right, (((left_dim,), (right_dim,)), ((), ())), preferred_element_type=F32
    )


def cost(us):
    return pl.CostEstimate(flops=1 + int(us * 1.15e9), bytes_accessed=1, transcendentals=0)


def params(mib=32):
    return pltpu.CompilerParams(vmem_limit_bytes=mib * 1024 * 1024)


def delta_kernel(rates, keys, values, gate, up, down, *refs):
    groups = len(GROUPS)
    mine, other, old = refs[:groups], refs[groups : 2 * groups], refs[2 * groups]
    r_ref, old_turned, k_ref, v_ref, columns, turned, sems = refs[2 * groups + 1 :]
    x, zl, core = coordinates()
    units = gate.shape[2] // NX
    half = units // NC
    early = keys.shape[0] // 2

    copies = [
        pltpu.make_async_copy(keys.at[:early], k_ref.at[:early], sems.at[0]),
        pltpu.make_async_copy(gate.at[0], columns.at[0], sems.at[1]),
        pltpu.make_async_copy(up.at[0], columns.at[1], sems.at[2]),
        pltpu.make_async_copy(keys.at[early:], k_ref.at[early:], sems.at[3]),
        pltpu.make_async_copy(values, v_ref, sems.at[4]),
        pltpu.make_async_copy(down.at[0], columns.at[2], sems.at[5]),
        pltpu.make_async_copy(rates, r_ref, sems.at[6]),
    ]
    for copy in copies:
        copy.start()
    copies[0].wait()
    parts = []
    for m in range(2):
        copies[1 + m].wait()
        parts.append(contract(columns[m], k_ref[:early], 0, 1))
    copies[3].wait()
    gate_in, up_in = (
        jnp.concatenate([part, contract(columns[m], k_ref[early:], 0, 1)], 1)
        for m, part in enumerate(parts)
    )
    copies[4].wait()
    copies[5].wait()
    copies[6].wait()
    k, v, r = k_ref[...], v_ref[...], r_ref[...]
    back = contract(columns[2], v, 0, 1)
    s = jax.nn.sigmoid(gate_in)
    act = gate_in * s
    rated = r * back
    turned[0] = (rated * up_in * s * (1.0 + gate_in * (1.0 - s))).astype(BF16)
    turned[1] = (rated * act).astype(BF16)
    turned[2] = (r * (act * up_in)).astype(BF16)
    pairs = [(c, i) for c in (1 - core, core) for i in range(NX)]
    rows = [
        pl.ds(pl.multiple_of((x + STEPS[i]) % NX * units + c * half, half), half) for c, i in pairs
    ]
    for m, tokens in enumerate((k, k, v)):
        sums = contract(jnp.concatenate([turned[m, part] for part in rows], 0), tokens, 1, 0).astype(BF16)
        for at, (_, i) in enumerate(pairs):
            g = next(g for g in range(groups) if i in GROUPS[g])
            (mine if at >= NX else other)[g][i - GROUPS[g][0], m] = sums[at * half : (at + 1) * half]
    block = pl.ds(pl.multiple_of(x * units, units), units)
    own = pl.ds(pl.multiple_of(zl * half, half), half)
    for m in range(3):
        old_turned[...] = columns[m, :, block].astype(F32).T
        old[m] = old_turned[own, :].astype(BF16)


def deltas(rates, arrays):
    count, width = arrays[0].shape
    n = arrays[2].shape[2]
    units = n // NX
    half = units // NC
    vmem = pl.BlockSpec(memory_space=pltpu.VMEM)
    out_shape = [jax.ShapeDtypeStruct((len(g), 3, half, width), BF16) for g in GROUPS * 2]
    out_shape.append(jax.ShapeDtypeStruct((3, half, width), BF16))
    return pl.pallas_call(
        delta_kernel,
        name="deltas",
        in_specs=[pl.BlockSpec(memory_space=pltpu.HBM)] + [pl.BlockSpec(memory_space=pl.ANY)] * len(arrays),
        out_specs=[vmem] * len(out_shape),
        out_shape=out_shape,
        scratch_shapes=[
            pltpu.VMEM((1, count), F32),
            pltpu.VMEM((units, width), F32),
            pltpu.VMEM((count, width), BF16),
            pltpu.VMEM((count, width), BF16),
            pltpu.VMEM((3, width, n), BF16),
            pltpu.VMEM((3, n, count), BF16),
            pltpu.SemaphoreType.DMA((7,)),
        ],
        compiler_params=params(50),
        cost_estimate=cost(DELTA_US),
    )(rates, *arrays)


def call(kernel, name, out_shape, *operands, us=0.0):
    vmem = pl.BlockSpec(memory_space=pltpu.VMEM)
    return pl.pallas_call(
        kernel,
        name=name,
        in_specs=[vmem] * len(operands),
        out_specs=jax.tree.map(lambda _: vmem, out_shape),
        out_shape=out_shape,
        compiler_params=params(),
        cost_estimate=cost(us),
    )(*operands)


def add_kernel(mine, other, *outs):
    for i, out in enumerate(outs):
        out[...] = (mine[i].astype(F32) + other[i].astype(F32)).astype(out.dtype)


def add_cores(mine, other):
    block = jax.ShapeDtypeStruct(mine.shape[1:], BF16)
    return call(add_kernel, "add_cores", [block] * mine.shape[0], mine, other)


def sum_kernel(*refs):
    sums = refs[0][...].astype(F32)
    for ref in refs[1:-1]:
        sums = sums + ref[...].astype(F32)
    refs[-1][...] = sums.astype(refs[-1].dtype)


def add_up(name, parts, us):
    return call(sum_kernel, name, jax.ShapeDtypeStruct(parts[0].shape, BF16), *parts, us=us)


def renorm_kernel(old, mine, other, *outs):
    n = outs[0].shape[1]
    _, _, core = coordinates()
    for m in range(3):
        halves = []
        for i in range(2):
            part = slice(i * n, (i + 1) * n)
            was = old[m, part, :].astype(F32)
            summed = was + (mine[m, part, :].astype(F32) + other[m, part, :].astype(F32))
            factor = jnp.sqrt(jnp.sum(was * was, axis=-1, keepdims=True)) / jnp.sqrt(
                jnp.sum(summed * summed, axis=-1, keepdims=True) + 1e-06
            )
            halves.append(summed * factor)
        for i, out in enumerate(outs):
            out[m] = jnp.where(core == i, halves[0], halves[1]).astype(BF16)


def join_kernel(*refs):
    out = refs[-1]
    at = 0
    for ref in refs[:-1]:
        n = ref.shape[1]
        out[:, at : at + n, :] = ref[...]
        at += n


def join(pieces):
    units = sum(p.shape[1] for p in pieces)
    out = jax.ShapeDtypeStruct((3, units, pieces[0].shape[2]), BF16)
    return call(join_kernel, "join", out, *pieces)


def render_kernel(cuts, count, added, *refs):
    rows, pieces, outs = refs[: len(cuts)], refs[len(cuts) : -count], refs[-count:]
    if added:
        *pieces, before = pieces
    gate, up, down = (jnp.concatenate([p[m] for p in pieces], 0) for m in range(3))
    q = jnp.concatenate([ref[lo:hi, :] for ref, (lo, hi) in zip(rows, cuts)], 0)
    gate_q = contract(q, gate, 1, 1)
    up_q = contract(q, up, 1, 1)
    hidden_q = (gate_q * jax.nn.sigmoid(gate_q) * up_q).astype(BF16)
    partial = contract(hidden_q, down, 1, 0)
    if added:
        partial = before[...] + partial
    n = outs[0].shape[0]
    for i, out in enumerate(outs):
        out[...] = partial[i * n : (i + 1) * n].astype(out.dtype)


def render(rows, pieces, outs, before=None):
    cuts = tuple((lo, hi) for _, lo, hi in rows)
    kernel = functools.partial(render_kernel, cuts, len(outs), before is not None)
    operands = [r[0] for r in rows] + list(pieces) + ([] if before is None else [before])
    return call(kernel, "render_rows", outs, *operands)


def merge_kernel(mid, relay_left, relay_right, to_right, to_left):
    half = to_right.shape[0]
    to_right[...] = (mid[:half] + relay_left[...].astype(F32)).astype(BF16)
    to_left[...] = (mid[half:] + relay_right[...].astype(F32)).astype(BF16)


def own_kernel(own, from_left, from_right, out):
    half = from_left.shape[0]
    out[:half] = own[:half] + from_right[...].astype(F32)
    out[half:] = own[half:] + from_left[...].astype(F32)


def total_kernel(own, last_left, last_right, out):
    half = last_left.shape[0]
    out[:half] = (own[:half] + last_left[...].astype(F32)).astype(BF16)
    out[half:] = (own[half:] + last_right[...].astype(F32)).astype(BF16)


def local(input_keys, input_values, token_rates, gate_weight, up_weight, down_weight, queries):
    arrays = (input_keys, input_values, gate_weight, up_weight, down_weight)
    rates = pltpu.with_memory_space_constraint(token_rates, pltpu.HBM)
    *parts, old = deltas(rates, arrays)
    chips = []
    for mine, other in zip(parts, parts[len(GROUPS) :]):
        chips += add_cores(mine, swap_core(other))
    got = [to_owner(chip, step) for chip, step in zip(chips, STEPS)]

    queries, *got[:2] = lax.optimization_barrier((queries, *got[:2]))
    half = queries.shape[0] // 2
    from_right, from_left = along_x(queries, -1), along_x(queries, 1)
    sums = add_up("sum_chips", got, SUM_US)
    out = jax.ShapeDtypeStruct((3, sums.shape[1] // 2, sums.shape[2]), BF16)
    news = call(renorm_kernel, "renorm", [out] * 2, old, sums, swap_core(sums))
    first = [along_z(new, 1) for new in news]
    second = [along_z(piece, 1) for piece in first]
    third = [along_z(piece, 1) for piece in second]
    far_top, far_low = along_x(from_right[:half], -1), along_x(from_left[half:], 1)
    third[1], far_top, far_low = lax.optimization_barrier((third[1], far_top, far_low))
    fourth = along_z(third[0], 1)
    near, last = join(first + second), join(third + [fourth])
    early, late = list(news) + [near, last], [swap_core(near), swap_core(last)]

    both, width = 2 * half, queries.shape[1]
    part = jax.ShapeDtypeStruct((half, width), BF16)
    wide = jax.ShapeDtypeStruct((both, width), F32)
    sets = [
        ([(far_top, 0, half), (far_low, 0, half)], [part] * 2),
        ([(from_right, half, both), (from_left, 0, half)], [part] * 2),
        ([(from_right, 0, half), (from_left, half, both)], [wide]),
        ([(queries, 0, both)], [wide]),
    ]
    (before,) = render(sets[0][0], early, [wide])
    late[1], before = lax.optimization_barrier((late[1], before))
    to_right, to_left = render(sets[0][0], late, sets[0][1], before)
    direct, (mid,), (own,) = (render(rows, early + late, outs) for rows, outs in sets[1:])
    relay_left, relay_right = along_x(to_right, 1), along_x(to_left, -1)
    from_left_x, from_right_x = along_x(direct[0], 1), along_x(direct[1], -1)
    to_right, to_left = call(merge_kernel, "merge", [part] * 2, mid, relay_left, relay_right)
    last_left, last_right = along_x(to_right, 1), along_x(to_left, -1)
    own = call(own_kernel, "own", wide, own, from_left_x, from_right_x, us=OWN_US)
    out = jax.ShapeDtypeStruct(own.shape, BF16)
    return call(total_kernel, "total", out, own, last_left, last_right)


def solution(mesh):
    return jax.shard_map(
        local,
        mesh=mesh,
        in_specs=(
            P("view", "head"),
            P("view", "head"),
            P("head", "view"),
            P("head", None, "render"),
            P("head", None, "render"),
            P("head", None, "render"),
            P(("view", "render"), "head"),
        ),
        out_specs=P(("view", "render"), "head"),
        check_vma=False,
    )
```
